256 devices in a mesh: seq: 8 (over z_hi, core), res: 32 (over y, x, z_lo).
Axes of the slice: x: 4, y: 4, z: 8 (z_hi: 4, z_lo: 2; z = z_hi * 2 + z_lo), core: 2. Of those that a mesh axis runs over, the one named last changes fastest.
Arguments:
- homolog_features: bfloat16 [16, 2048, 256], P('seq', 'res'), may hold values from -6 to 6
- couple_features: bfloat16 [2048, 2048, 128], P('res', 'seq'), may hold values from -40 to 40
- result_adjoint: bfloat16 [16, 2048, 256], P('seq', 'res'), may hold values from -6 to 6
- asking_projection: bfloat16 [256, 256], replicated, may hold values from -0.375 to 0.375
- lookup_projection: bfloat16 [256, 256], replicated, may hold values from -0.375 to 0.375
- content_projection: bfloat16 [256, 256], replicated, may hold values from -0.375 to 0.375
- sigmoid_projection: bfloat16 [256, 256], replicated, may hold values from -0.375 to 0.375
- sigmoid_shift_vector: float32 [256], replicated, may hold values from -4 to 4
- couple_to_heads_map: bfloat16 [128, 8], replicated, may hold values from -0.5 to 0.5
- result_projection: bfloat16 [256, 256], replicated, may hold values from -0.375 to 0.375
Outputs:
- homolog_derivative: bfloat16 [16, 2048, 256], P('seq', 'res')
- couple_derivative: bfloat16 [2048, 2048, 128], P('res', 'seq')
The draws below stay inside these ranges and needn't reach their ends.
All inputs are finite; a program needn't handle non-finite values.
Results may differ from the reference program's by a relative error of at most 0.011.
Values may be sent and summed in bfloat16 or wider, within the bound.
A program may use at most 128 MiB of HBM per device.

```python
import jax
import jax.numpy as jnp
from jax import lax

FEATURE_DEPTH = 256
HEAD_AMOUNT = 8
HEAD_DEPTH = 32
CZ = 128
RES_DEV = 64
HOMOLOG_AMOUNT = 16
POSITION_AMOUNT = 2048


def shared_signs(key):
    flips = jax.random.bernoulli(jax.random.fold_in(key, 11), 0.5, (CZ,))
    return jnp.where(flips, 1.0, -1.0).astype(jnp.float32)


def draw_couple_to_heads_map(key, part):
    signs = shared_signs(key)
    key = jax.random.fold_in(key, 1)
    magnitude = jnp.abs(jax.random.normal(key, (CZ, HEAD_AMOUNT), jnp.float32))
    value_rows = signs[:, None] * magnitude * CZ ** (-0.5)
    return jnp.clip(value_rows, -0.5, 0.5).astype(jnp.bfloat16)


def draw_couple_features(key, part):
    key = jax.random.fold_in(key, 2)
    key_base = jax.random.fold_in(key, 0)
    base = jax.random.normal(key_base, (POSITION_AMOUNT, POSITION_AMOUNT, CZ), jnp.float32)
    return jnp.clip(base, -40.0, 40.0).astype(jnp.bfloat16)


def block_levels(own_key, shape, pieces, least, top_value):
    loudness, own = 1.0, jax.random.fold_in(own_key, 6)
    for position, parts in pieces:
        draws = jnp.exp(jax.random.uniform(jax.random.fold_in(own, position), (parts,), jnp.float32, least / len(pieces), top_value / len(pieces)))
        loudness = loudness * jnp.repeat(draws, shape[position] // parts).reshape([-1 if axis == position else 1 for axis in range(len(shape))])
    return loudness


def scatter_about(rng, dims, spread, reach, cuts=(), held_as=jnp.bfloat16):
    drawn = spread * jax.random.normal(rng, dims, jnp.float32)
    if cuts:
        drawn = drawn * block_levels(rng, dims, cuts, -0.22, 0.18)
    return jnp.clip(drawn, -reach, reach).astype(held_as)


def setup_inputs(seed: int = 0) -> dict:
    key_list = jax.random.split(jax.random.key(seed), 11)
    homolog_features = scatter_about(key_list[0], (HOMOLOG_AMOUNT, POSITION_AMOUNT, FEATURE_DEPTH), 1.0, 6.0, ((0, 8), (1, 32)))
    couple_features = draw_couple_features(jax.random.fold_in(key_list[10], 71), 0)
    result_adjoint = scatter_about(key_list[2], (HOMOLOG_AMOUNT, POSITION_AMOUNT, FEATURE_DEPTH), 1.0, 6.0, ((0, 8), (1, 32)))
    asking_projection = scatter_about(key_list[3], (FEATURE_DEPTH, HEAD_AMOUNT * HEAD_DEPTH), FEATURE_DEPTH ** -0.5, 0.375)
    lookup_projection = scatter_about(key_list[4], (FEATURE_DEPTH, HEAD_AMOUNT * HEAD_DEPTH), FEATURE_DEPTH ** -0.5, 0.375)
    content_projection = scatter_about(key_list[5], (FEATURE_DEPTH, HEAD_AMOUNT * HEAD_DEPTH), FEATURE_DEPTH ** -0.5, 0.375)
    sigmoid_projection = scatter_about(key_list[6], (FEATURE_DEPTH, HEAD_AMOUNT * HEAD_DEPTH), FEATURE_DEPTH ** -0.5, 0.375)
    sigmoid_shift_vector = scatter_about(key_list[7], (HEAD_AMOUNT * HEAD_DEPTH,), 1.0, 4.0, (), jnp.float32)
    couple_to_heads_map = draw_couple_to_heads_map(jax.random.fold_in(key_list[10], 71), 0)
    result_projection = scatter_about(key_list[9], (HEAD_AMOUNT * HEAD_DEPTH, FEATURE_DEPTH), (HEAD_AMOUNT * HEAD_DEPTH) ** -0.5, 0.375)
    return {"homolog_features": homolog_features, "couple_features": couple_features, "result_adjoint": result_adjoint, "asking_projection": asking_projection, "lookup_projection": lookup_projection, "content_projection": content_projection, "sigmoid_projection": sigmoid_projection, "sigmoid_shift_vector": sigmoid_shift_vector, "couple_to_heads_map": couple_to_heads_map, "result_projection": result_projection}


def reference(homolog_features, couple_features, result_adjoint, asking_projection, lookup_projection, content_projection, sigmoid_projection, sigmoid_shift_vector, couple_to_heads_map, result_projection):
    inner = HEAD_AMOUNT * HEAD_DEPTH
    logit_scale = HEAD_DEPTH ** -0.5
    weight_bias = couple_to_heads_map.astype(jnp.float32)
    blocks = couple_features.reshape(POSITION_AMOUNT // RES_DEV, RES_DEV, POSITION_AMOUNT, CZ)
    bias_parts = lax.map(lambda block: jnp.einsum("ijc,ch->hij", block.astype(jnp.float32), weight_bias), blocks)
    bias = bias_parts.transpose(1, 0, 2, 3).reshape(HEAD_AMOUNT, POSITION_AMOUNT, POSITION_AMOUNT)
    key_back = jnp.concatenate([lookup_projection.T, content_projection.T], 0).astype(jnp.float32)

    def per_homolog(carry, layer_inputs):
        alignment_rows, row_gradient = layer_inputs
        query_rows = (jnp.dot(alignment_rows, asking_projection, preferred_element_type=jnp.float32) * logit_scale).astype(jnp.bfloat16)
        key_rows = jnp.dot(alignment_rows, lookup_projection, preferred_element_type=jnp.float32).astype(jnp.bfloat16)
        value_rows = jnp.dot(alignment_rows, content_projection, preferred_element_type=jnp.float32).astype(jnp.bfloat16)
        gate_values = jax.nn.sigmoid(jnp.dot(alignment_rows, sigmoid_projection, preferred_element_type=jnp.float32) + sigmoid_shift_vector)
        q_heads = query_rows.reshape(POSITION_AMOUNT, HEAD_AMOUNT, HEAD_DEPTH).astype(jnp.float32)
        k_heads = key_rows.reshape(POSITION_AMOUNT, HEAD_AMOUNT, HEAD_DEPTH).astype(jnp.float32)
        v_heads = value_rows.reshape(POSITION_AMOUNT, HEAD_AMOUNT, HEAD_DEPTH).astype(jnp.float32)
        scores = jnp.einsum("ihd,jhd->hij", q_heads, k_heads) + bias
        probs = jax.nn.softmax(scores, axis=-1)
        probs_b = probs.astype(jnp.bfloat16).astype(jnp.float32)
        attended = jnp.einsum("hij,jhd->ihd", probs_b, v_heads).reshape(POSITION_AMOUNT, inner)
        d_gated = jnp.dot(row_gradient, result_projection.T, preferred_element_type=jnp.float32)
        d_attended = (d_gated * gate_values).astype(jnp.bfloat16)
        d_gate_pre = (d_gated * attended * gate_values * (1.0 - gate_values)).astype(jnp.bfloat16)
        d_att_heads = d_attended.reshape(POSITION_AMOUNT, HEAD_AMOUNT, HEAD_DEPTH).astype(jnp.float32)
        d_probs = jnp.einsum("ihd,jhd->hij", d_att_heads, v_heads)
        delta = jnp.sum(probs * d_probs, axis=-1, keepdims=True)
        d_scores = probs * (d_probs - delta)
        d_scores_b = d_scores.astype(jnp.bfloat16).astype(jnp.float32)
        d_values = jnp.einsum("hij,ihd->jhd", probs_b, d_att_heads).reshape(POSITION_AMOUNT, inner)
        d_keys = jnp.einsum("hij,ihd->jhd", d_scores_b, q_heads).reshape(POSITION_AMOUNT, inner)
        d_query = (jnp.einsum("hij,jhd->ihd", d_scores_b, k_heads) * logit_scale).astype(jnp.bfloat16).reshape(POSITION_AMOUNT, inner)
        local_part = jnp.dot(d_query, asking_projection.T, preferred_element_type=jnp.float32)
        local_part = local_part + jnp.dot(d_gate_pre, sigmoid_projection.T, preferred_element_type=jnp.float32)
        key_part = jnp.dot(jnp.concatenate([d_keys, d_values], 1), key_back, precision=lax.Precision.HIGHEST)
        return carry + d_scores, (local_part + key_part).astype(jnp.bfloat16)

    beginning_position = jnp.zeros((HEAD_AMOUNT, POSITION_AMOUNT, POSITION_AMOUNT), jnp.float32)
    adjoint_for_shift, homolog_derivative = lax.scan(per_homolog, beginning_position, (homolog_features, result_adjoint))
    grad_blocks = adjoint_for_shift.reshape(HEAD_AMOUNT, POSITION_AMOUNT // RES_DEV, RES_DEV, POSITION_AMOUNT).transpose(1, 0, 2, 3)
    pair_parts = lax.map(lambda block: jnp.einsum("hij,ch->ijc", block, weight_bias, precision=lax.Precision.HIGHEST).astype(jnp.bfloat16), grad_blocks)
    couple_derivative = pair_parts.reshape(POSITION_AMOUNT, POSITION_AMOUNT, CZ)
    return homolog_derivative, couple_derivative
```

```python
import functools

import jax
import jax.numpy as jnp
from jax import lax
from jax.experimental import pallas as pl
from jax.experimental.pallas import tpu as pltpu
from jax.sharding import PartitionSpec as P

F32, BF16 = jnp.float32, jnp.bfloat16
MESH = pl.DeviceIdType.MESH
ORDER = (0, 1, 3, 2)
NT = (((1,), (1,)), ((), ()))
TN = (((0,), (0,)), ((), ()))
VMEM_LIMIT = 60 * 1024 * 1024


def dot(a, b, dims=(((1,), (0,)), ((), ()))):
    return lax.dot_general(a, b, dims, preferred_element_type=F32)


def coords():
    s, r = lax.axis_index("seq"), lax.axis_index("res")
    return (
        lax.div(s, 2),
        lax.rem(s, 2),
        lax.div(r, 8),
        lax.rem(lax.div(r, 2), 4),
        lax.rem(r, 2),
    )


def device(zh, c, y, x, zl):
    return (zh * 2 + c, y * 8 + x * 2 + zl)


def mod4(v):
    return lax.rem(v + 8, 4)


def remote(src, dst, ssem, rsem, dev):
    return pltpu.make_async_remote_copy(
        src_ref=src, dst_ref=dst, send_sem=ssem, recv_sem=rsem, device_id=dev, device_id_type=MESH
    )


def entry_barrier(devices):
    barrier = pltpu.get_barrier_semaphore()
    for dev in devices:
        pl.semaphore_signal(barrier, inc=1, device_id=dev, device_id_type=MESH)
    pl.semaphore_wait(barrier, len(devices))


def slab_partners(zh, c, y, x, zl):
    return (
        [device(mod4(zh + d), c, y, x, zl) for d in (1, 2, 3)]
        + [device(zh, c, mod4(y + d), x, zl) for d in (1, 3)]
        + [device(zh, c, y, mod4(x + d), zl) for d in (1, 3)]
        + [device(zh, c, y, x, 1 - zl)]
    )


def gather_kernel(
    feat, adj, qf, ag, kv, zs, zr, as_, ar, ys, yr, ls, lr, xs, xr, x2s, x2r
):
    zh, c, y, x, zl = coords()
    entry_barrier(slab_partners(zh, c, y, x, zl))
    role = mod4(y - zh)
    jb = x * 2 + zl
    left, right = mod4(x - 1), mod4(x + 1)
    dev_left, dev_right = device(zh, c, y, left, zl), device(zh, c, y, right, zl)
    dev_up, dev_down = device(zh, c, mod4(y + 1), x, zl), device(zh, c, mod4(y - 1), x, zl)
    dev_zl = device(zh, c, y, x, 1 - zl)

    def zcopy(src, dst, ssem, rsem, d):
        return remote(
            src, dst.at[pl.ds(2 * zh, 2)], ssem.at[d - 1], rsem.at[d - 1],
            device(mod4(zh + d), c, y, x, zl),
        )

    def zwait(src, dst, ssem, rsem, d):
        remote(
            src, dst.at[pl.ds(2 * mod4(zh - d), 2)], ssem.at[d - 1], rsem.at[d - 1],
            device(mod4(zh + d), c, y, x, zl),
        ).wait_recv()

    for d in (1, 3, 2):
        zcopy(feat, qf, zs, zr, d).start()
    for d in (1, 3, 2):
        zcopy(adj, ag, as_, ar, d).start()
    qf[pl.ds(2 * zh, 2)] = feat[...]
    ag[pl.ds(2 * zh, 2)] = adj[...]

    def chunk(q):
        return 2 * mod4(zh - ORDER[q])

    def y_first(q, which):
        here = kv.at[pl.ds(chunk(q), 2), jb]
        return remote(
            qf.at[pl.ds(chunk(q), 2)], here, ys.at[q, which], yr.at[q, 0], (dev_up, dev_down)[which]
        )

    def y_half(q, which):
        here = kv.at[chunk(q) + which, jb]
        return remote(here, here, ys.at[q, which], yr.at[q, which], (dev_up, dev_down)[which])

    def z_pair(q):
        here = kv.at[pl.ds(chunk(q), 2), jb]
        return remote(here, here, ls.at[q], lr.at[q], dev_zl)

    def z_pair_in(q):
        here = kv.at[pl.ds(chunk(q), 2), x * 2 + 1 - zl]
        return remote(here, here, ls.at[q], lr.at[q], dev_zl)

    def x_first(q, which, owner):
        here = kv.at[pl.ds(chunk(q), 2), pl.ds(2 * owner, 2)]
        return remote(here, here, xs.at[q, which], xr.at[q, which], (dev_right, dev_left)[which])

    def x_half(q, which, owner):
        here = kv.at[chunk(q) + which, pl.ds(2 * owner, 2)]
        return remote(here, here, x2s.at[q, which], x2r.at[q, which], (dev_right, dev_left)[which])

    def stage_y(q):
        d = ORDER[q]
        if d:
            zwait(feat, qf, zs, zr, d)

        @pl.when(role == 0)
        def _():
            y_first(q, 0).start()
            y_first(q, 1).start()
            kv[pl.ds(chunk(q), 2), jb] = qf[pl.ds(chunk(q), 2)]

        @pl.when(role == 1)
        def _():
            y_first(q, 0).wait_recv()
            y_half(q, 0).start()

        @pl.when(role == 3)
        def _():
            y_first(q, 0).wait_recv()
            y_half(q, 1).start()

        @pl.when(role == 2)
        def _():
            y_half(q, 0).wait_recv()
            y_half(q, 1).wait_recv()

        z_pair(q).start()

    def stage_x(q):
        z_pair_in(q).wait_recv()
        x_first(q, 0, x).start()
        x_first(q, 1, x).start()

    def stage_x2(q):
        x_first(q, 0, left).wait_recv()
        x_half(q, 0, left).start()
        x_first(q, 1, right).wait_recv()
        x_half(q, 1, right).start()

    def stage_end(q):
        x_half(q, 0, mod4(x + 2)).wait_recv()
        x_half(q, 1, mod4(x + 2)).wait_recv()

    for t in range(7):
        for lag, stage in enumerate((stage_y, stage_x, stage_x2, stage_end)):
            if 0 <= t - lag < 4:
                stage(t - lag)

    for d in (1, 3, 2):
        zwait(adj, ag, as_, ar, d)
        zcopy(feat, qf, zs, zr, d).wait_send()
        zcopy(adj, ag, as_, ar, d).wait_send()
    for q in range(4):

        @pl.when(role == 0)
        def _():
            y_first(q, 0).wait_send()
            y_first(q, 1).wait_send()

        @pl.when(role == 1)
        def _():
            y_half(q, 0).wait_send()

        @pl.when(role == 3)
        def _():
            y_half(q, 1).wait_send()

        z_pair(q).wait_send()
        for which in (0, 1):
            x_first(q, which, x).wait_send()
            x_half(q, which, x).wait_send()


def head_mask(rows):
    lane = lax.broadcasted_iota(jnp.int32, (rows, 256), 1)
    return [(lane >= 32 * h) & (lane < 32 * h + 32) for h in range(8)]


def spread_map(rep, out):
    row = lax.broadcasted_iota(jnp.int32, (128, 128), 0)
    wide = rep.astype(F32)
    for i in range(16):
        out[:, i * 128 : (i + 1) * 128] = jnp.where(lax.rem(row, 16) == i, wide, 0.0).astype(BF16)


def attention_kernel(
    pair, qf, ag, kv, wq, wk, wv, wg, bg, wo, wback, rep,
    part, ipart, db,
    bias, dbias, pbuf, dpbuf, kbuf, vbuf, qbd, dabd, fac, sbuf, pb, dsb, wexp, st, stout, stin, ab, dbin,
    bs, br, ss, sr, es, er,
):
    zh, c, y, x, zl = coords()
    other = device(zh, 1 - c, y, x, zl)
    peers = [device(mod4(zh + d), c, y, x, zl) for d in (1, 2, 3)]
    entry_barrier([other] + peers)

    spread_map(rep[...], wexp)
    for g in range(4):
        total = jnp.zeros((128, 256), F32)
        for p in range(8):
            i = 16 * g + 2 * p
            both = jnp.concatenate([pair[i], pair[i + 1]], axis=1)
            total += dot(wexp[:, p * 256 : (p + 1) * 256], both, NT)
        for h in range(8):
            bias[c, h * 64 + 16 * g : h * 64 + 16 * g + 16, :] = total[h * 16 : h * 16 + 16]
    swap = remote(bias.at[c], bias.at[c], bs, br, other)
    swap.start()

    masks = head_mask(64)

    def query_side(n, carry):
        rows = qf[n]
        q = (dot(rows, wq[...]) * (32**-0.5)).astype(BF16)
        gate = jax.nn.sigmoid(dot(rows, wg[...]) + bg[...])
        dg = dot(ag[n], wo[...], NT)
        da = (dg * gate).astype(BF16)
        fac[n] = dg * gate * (1.0 - gate)
        for h in range(8):
            qbd[n, h * 64 : h * 64 + 64, :] = jnp.where(masks[h], q.astype(F32), 0.0).astype(BF16)
            dabd[n, h * 64 : h * 64 + 64, :] = jnp.where(masks[h], da.astype(F32), 0.0).astype(BF16)
        k = dot(kv[n], wk[...]).astype(BF16)
        v = dot(kv[n], wv[...]).astype(BF16)
        kbuf[n] = k
        vbuf[n] = v
        return carry

    lax.fori_loop(0, 8, query_side, 0)
    remote(bias.at[1 - c], bias.at[1 - c], bs, br, other).wait_recv()

    lane = lax.broadcasted_iota(jnp.int32, (64, 128), 1)

    def first(n, carry):
        sbuf[...] = dot(qbd[n], kbuf[n], NT)
        dpbuf[n] = dot(dabd[n], vbuf[n], NT)
        for h in range(8):
            rows = pl.ds(h * 64, 64)
            s0 = sbuf[rows, 0:256] + bias[0, rows, :]
            s1 = sbuf[rows, 256:512] + bias[1, rows, :]
            top = jnp.max(jnp.maximum(s0, s1), axis=1, keepdims=True)
            p0, p1 = jnp.exp(s0 - top), jnp.exp(s1 - top)
            pbuf[n, rows, 0:256] = p0
            pbuf[n, rows, 256:512] = p1
            total = jnp.sum(p0 + p1, axis=1, keepdims=True)
            mixed = jnp.sum(
                p0 * dpbuf[n, rows, 0:256] + p1 * dpbuf[n, rows, 256:512], axis=1, keepdims=True
            )
            old = jnp.where(lane == n, top, st[rows, :])
            old = jnp.where(lane == n + 8, total, old)
            st[rows, :] = jnp.where(lane == n + 16, mixed, old)
        return carry

    st[...] = jnp.zeros_like(st)
    lax.fori_loop(0, 8, first, 0)

    stout[...] = st[...].T[0:24]
    for d in (1, 2, 3):
        remote(stout, stin.at[d - 1], ss.at[d - 1], sr.at[d - 1], peers[d - 1]).start()
    for d in (1, 2, 3):
        remote(stout, stin.at[d - 1], ss.at[d - 1], sr.at[d - 1], peers[d - 1]).wait()
    own_top = stout[0:8]
    tops = [own_top] + [stin[d, 0:8] for d in range(3)]
    top = jnp.maximum(jnp.maximum(tops[0], tops[1]), jnp.maximum(tops[2], tops[3]))
    own_scale = jnp.exp(own_top - top)
    total, mixed = own_scale * stout[8:16], own_scale * stout[16:24]
    for d in range(3):
        scale = jnp.exp(tops[d + 1] - top)
        total += scale * stin[d, 8:16]
        mixed += scale * stin[d, 16:24]
    ab[...] = jnp.concatenate(
        [own_scale / total, mixed / total, jnp.zeros((112, 512), F32)], axis=0
    ).T

    dbias[...] = jnp.zeros_like(dbias)

    def second(n, carry):
        for h in range(8):
            rows = pl.ds(h * 64, 64)
            both = ab[rows, :]
            a = jnp.sum(jnp.where(lane == n, both, 0.0), axis=1, keepdims=True)
            delta = jnp.sum(jnp.where(lane == n + 8, both, 0.0), axis=1, keepdims=True)
            for half in (0, 1):
                cols = slice(half * 256, half * 256 + 256)
                probs = pbuf[n, rows, cols] * a
                pb[rows, cols] = probs.astype(BF16)
                ds = probs * (dpbuf[n, rows, cols] - delta)
                dsb[rows, cols] = ds.astype(BF16)
                dbias[half, rows, :] += ds
        att_all = dot(pb[...], vbuf[n])
        dq_all = dot(dsb[...], kbuf[n])
        att, dq = jnp.zeros((64, 256), F32), jnp.zeros((64, 256), F32)
        for h in range(8):
            att += jnp.where(masks[h], att_all[h * 64 : h * 64 + 64], 0.0)
            dq += jnp.where(masks[h], dq_all[h * 64 : h * 64 + 64], 0.0)
        dq = (dq * (32**-0.5)).astype(BF16)
        dgp = (fac[n] * att).astype(BF16)
        ipart[n] = dot(dq, wq[...], NT) + dot(dgp, wg[...], NT)
        dk = dot(qbd[n], dsb[...], TN).astype(BF16)
        dv = dot(dabd[n], pb[...], TN).astype(BF16)
        part[n] = (dot(dk, wback[0:256], TN) + dot(dv, wback[256:512], TN)).astype(BF16)
        return carry

    lax.fori_loop(0, 8, second, 0)

    back = remote(dbias.at[1 - c], dbin, es, er, other)
    back.start()
    back.wait()
    db[...] = dbias[c] + dbin[...]
    swap.wait_send()


def couple_kernel(db, rep, out, wexp):
    spread_map(rep[...], wexp)
    rows = db[...].reshape(128, 256)
    high = rows.astype(BF16)
    low = (rows - high.astype(F32)).astype(BF16)
    both = jnp.concatenate([high, low], axis=0).T
    for p in range(8):
        w = wexp[:, p * 256 : (p + 1) * 256]
        res = dot(both, jnp.concatenate([w, w], axis=0)).astype(BF16)
        out[2 * p] = res[:, 0:128]
        out[2 * p + 1] = res[:, 128:256]


def reduce_kernel(
    part, ipart, out,
    acc, tosend, in_x2, in_x, in_l, in_y, zout, zin, hop1, hop2, hopl, hopy,
    x2s, x2r, xs, xr, ls, lr, ys, yr, zs, zr,
):
    zh, c, y, x, zl = coords()
    entry_barrier(slab_partners(zh, c, y, x, zl))
    role = mod4(y - zh)
    left, right, far = mod4(x - 1), mod4(x + 1), mod4(x + 2)
    dev_left, dev_right = device(zh, c, y, left, zl), device(zh, c, y, right, zl)
    dev_up, dev_down = device(zh, c, mod4(y + 1), x, zl), device(zh, c, mod4(y - 1), x, zl)
    dev_zl = device(zh, c, y, x, 1 - zl)
    sides = (dev_right, dev_left)
    near = (right, left)

    def chunk(q):
        return 2 * mod4(zh - ORDER[3 - q])

    def x_half(q, which):
        return remote(
            part.at[chunk(q) + which, pl.ds(2 * far, 2)], in_x2.at[q, which],
            x2s.at[q, which], x2r.at[q, which], sides[which],
        )

    def x_first(q, which):
        return remote(
            hop1.at[q, which], in_x.at[q, which], xs.at[q, which], xr.at[q, which], sides[which]
        )

    def z_pair(q):
        return remote(hopl.at[q], in_l.at[q], ls.at[q], lr.at[q], dev_zl)

    def y_half(q, which):
        return remote(
            hopy.at[q, which], in_y.at[q, 0, which], ys.at[q, which], yr.at[q, 0],
            (dev_down, dev_up)[which],
        )

    def y_first(q, which):
        return remote(
            hopy.at[q], in_y.at[q, which], ys.at[q, 0], yr.at[q, which], (dev_down, dev_up)[which]
        )

    def z_out(q):
        d = ORDER[3 - q]
        return remote(
            zout.at[q], zin.at[q], zs.at[q], zr.at[q], device(mod4(zh - d), c, y, x, zl)
        )

    def stage_x(q):
        for which in (0, 1):
            x_half(q, which).start()

    def stage_x2(q):
        for which in (0, 1):
            x_half(q, which).wait_recv()
            n = chunk(q)
            mine = part[pl.ds(n, 2), pl.ds(2 * near[which], 2)].astype(F32)
            got = in_x2[q, which].astype(F32)
            if which == 0:
                hop1[q, which, 0] = (mine[0] + got).astype(BF16)
                hop1[q, which, 1] = mine[1].astype(BF16)
            else:
                hop1[q, which, 0] = mine[0].astype(BF16)
                hop1[q, which, 1] = (mine[1] + got).astype(BF16)
            x_first(q, which).start()

    def stage_l(q):
        for which in (0, 1):
            x_first(q, which).wait_recv()
        n = chunk(q)

        def total(b):
            return (
                part[pl.ds(n, 2), 2 * x + b].astype(F32)
                + in_x[q, 0, :, b].astype(F32)
                + in_x[q, 1, :, b].astype(F32)
            )

        acc[q] = total(zl)
        hopl[q] = total(1 - zl).astype(BF16)
        z_pair(q).start()

    def stage_y(q):
        z_pair(q).wait_recv()
        acc[q] = acc[q] + in_l[q].astype(F32)

        @pl.when(role == 2)
        def _():
            hopy[q] = acc[q].astype(BF16)
            y_half(q, 0).start()
            y_half(q, 1).start()

    def stage_y2(q):
        @pl.when(role == 1)
        def _():
            y_half(q, 0).wait_recv()
            acc[q, 0] = acc[q, 0] + in_y[q, 0, 0].astype(F32)
            hopy[q] = acc[q].astype(BF16)
            y_first(q, 0).start()

        @pl.when(role == 3)
        def _():
            y_half(q, 1).wait_recv()
            acc[q, 1] = acc[q, 1] + in_y[q, 0, 1].astype(F32)
            hopy[q] = acc[q].astype(BF16)
            y_first(q, 1).start()

    def stage_z(q):
        n = chunk(q)
        mine = ipart[pl.ds(n, 2)]

        @pl.when(role == 0)
        def _():
            y_first(q, 0).wait_recv()
            y_first(q, 1).wait_recv()
            acc[q] = (
                mine + acc[q] + in_y[q, 0].astype(F32) + in_y[q, 1].astype(F32)
            )

        @pl.when(role != 0)
        def _():
            acc[q] = mine

        if ORDER[3 - q]:
            zout[q] = acc[q].astype(BF16)
            z_out(q).start()

    for t in range(9):
        for lag, stage in enumerate((stage_x, stage_x2, stage_l, stage_y, stage_y2, stage_z)):
            if 0 <= t - lag < 4:
                stage(t - lag)

    total = acc[3]
    for q in range(3):
        z_out(q).wait_recv()
        total += zin[q].astype(F32)
    out[...] = total.astype(BF16)

    for q in range(4):
        for which in (0, 1):
            x_half(q, which).wait_send()
            x_first(q, which).wait_send()
        z_pair(q).wait_send()

        @pl.when(role == 2)
        def _():
            y_half(q, 0).wait_send()
            y_half(q, 1).wait_send()

        @pl.when(role == 1)
        def _():
            y_first(q, 0).wait_send()

        @pl.when(role == 3)
        def _():
            y_first(q, 1).wait_send()

        if q < 3:
            z_out(q).wait_send()


VM = pl.BlockSpec(memory_space=pltpu.VMEM)
DMA = pltpu.SemaphoreType.DMA


def params(cid):
    return pltpu.CompilerParams(
        collective_id=cid, has_side_effects=True, vmem_limit_bytes=VMEM_LIMIT
    )


def per_device(feat, pair, adj, wq, wk, wv, wg, bg, wch, wo):
    rep = jnp.repeat(wch.T, 16, axis=0)
    wback = jnp.concatenate([wk.T, wv.T], axis=0)
    sds = jax.ShapeDtypeStruct
    qf, ag, kv = pl.pallas_call(
        gather_kernel,
        out_shape=(
            sds((8, 64, 256), BF16), sds((8, 64, 256), BF16), sds((8, 8, 64, 256), BF16)
        ),
        in_specs=[VM] * 2,
        out_specs=(VM,) * 3,
        scratch_shapes=[DMA((3,))] * 4
        + [DMA((4, 2))] * 2 + [DMA((4,))] * 2 + [DMA((4, 2))] * 4,
        compiler_params=params(0),
        name="gather",
    )(feat, adj)
    part, ipart, db = pl.pallas_call(
        attention_kernel,
        out_shape=(sds((8, 512, 256), BF16), sds((8, 64, 256), F32), sds((512, 256), F32)),
        in_specs=[VM] * 12,
        out_specs=(VM,) * 3,
        scratch_shapes=[
            pltpu.VMEM((2, 512, 256), F32),
            pltpu.VMEM((2, 512, 256), F32),
            pltpu.VMEM((8, 512, 512), F32),
            pltpu.VMEM((8, 512, 512), F32),
            pltpu.VMEM((8, 512, 256), BF16),
            pltpu.VMEM((8, 512, 256), BF16),
            pltpu.VMEM((8, 512, 256), BF16),
            pltpu.VMEM((8, 512, 256), BF16),
            pltpu.VMEM((8, 64, 256), F32),
            pltpu.VMEM((512, 512), F32),
            pltpu.VMEM((512, 512), BF16),
            pltpu.VMEM((512, 512), BF16),
            pltpu.VMEM((128, 2048), BF16),
            pltpu.VMEM((512, 128), F32),
            pltpu.VMEM((24, 512), F32),
            pltpu.VMEM((3, 24, 512), F32),
            pltpu.VMEM((512, 128), F32),
            pltpu.VMEM((512, 256), F32),
            DMA, DMA, DMA((3,)), DMA((3,)), DMA, DMA,
        ],
        compiler_params=params(1),
        name="attention",
    )(pair, qf, ag, kv.reshape(8, 512, 256), wq, wk, wv, wg, bg.reshape(1, 256), wo, wback, rep)
    homolog = pl.pallas_call(
        reduce_kernel,
        out_shape=sds((2, 64, 256), BF16),
        in_specs=[VM] * 2,
        out_specs=VM,
        scratch_shapes=[
            pltpu.VMEM((4, 2, 64, 256), F32),
            pltpu.VMEM((8, 128), F32),
            pltpu.VMEM((4, 2, 2, 64, 256), BF16),
            pltpu.VMEM((4, 2, 2, 2, 64, 256), BF16),
            pltpu.VMEM((4, 2, 64, 256), BF16),
            pltpu.VMEM((4, 2, 2, 64, 256), BF16),
            pltpu.VMEM((3, 2, 64, 256), BF16),
            pltpu.VMEM((3, 2, 64, 256), BF16),
            pltpu.VMEM((4, 2, 2, 2, 64, 256), BF16),
            pltpu.VMEM((8, 128), F32),
            pltpu.VMEM((4, 2, 64, 256), BF16),
            pltpu.VMEM((4, 2, 64, 256), BF16),
            DMA((4, 2)), DMA((4, 2)), DMA((4, 2)), DMA((4, 2)),
            DMA((4,)), DMA((4,)), DMA((4, 2)), DMA((4, 2)), DMA((3,)), DMA((3,)),
        ],
        compiler_params=params(2),
        name="reduce",
    )(part.reshape(8, 8, 64, 256), ipart)
    couple = pl.pallas_call(
        couple_kernel,
        out_shape=sds((64, 256, 128), BF16),
        grid=(4,),
        in_specs=[
            pl.BlockSpec((8, 16, 256), lambda g: (0, g, 0)),
            pl.BlockSpec((128, 128), lambda g: (0, 0)),
        ],
        out_specs=pl.BlockSpec((16, 256, 128), lambda g: (g, 0, 0)),
        scratch_shapes=[pltpu.VMEM((128, 2048), BF16)],
        compiler_params=pltpu.CompilerParams(vmem_limit_bytes=VMEM_LIMIT),
        name="couple",
    )(db.reshape(8, 64, 256), rep)
    return homolog, couple


def solution(mesh):
    in_specs = (
        P("seq", "res", None), P("res", "seq", None), P("seq", "res", None),
        P(), P(), P(), P(), P(), P(), P(),
    )
    out_specs = (P("seq", "res", None), P("res", "seq", None))
    return jax.shard_map(
        per_device, mesh=mesh, in_specs=in_specs, out_specs=out_specs, check_vma=False
    )
```

```python
import contextlib

import jax
import jax.numpy as jnp
from jax import lax
from jax.experimental import pallas as pl
from jax.experimental.pallas import tpu as pltpu
from jax.sharding import PartitionSpec as P

F32, BF16 = jnp.float32, jnp.bfloat16
MESH = pl.DeviceIdType.MESH
NT = (((1,), (1,)), ((), ()))
TN = (((0,), (0,)), ((), ()))
VMEM_LIMIT = 61 * 1024 * 1024
SCALE = 32**-0.5
TRACE = False


def scope(name):
    return jax.named_scope(name) if TRACE else contextlib.nullcontext()


def dot(a, b, dims=(((1,), (0,)), ((), ()))):
    return lax.dot_general(a, b, dims, preferred_element_type=F32)


def mod4(v):
    return lax.rem(v + 8, 4)


def gray(k):
    return k + lax.div(k, 2) - 2 * lax.div(k, 3)


def spread_map(rep, out):
    row = lax.broadcasted_iota(jnp.int32, (128, 128), 0)
    for i in range(16):
        out[:, i * 128 : (i + 1) * 128] = jnp.where(lax.rem(row, 16) == i, rep, 0.0).astype(BF16)


def kernel(
    feat, pair_in, adj, wq, wk, wv, wg, bg, wch, wo,
    out, couple,
    pair, qf, ag, kv, bias, dbias, dbin, pbuf, dpbuf, kbuf, vbuf, qbd, dabd, fac, sbuf, pb, dsb, wexp,
    stout, stin, ipart, part, in_x, acc, hopl, in_l, hopy, in_y, zout, zin,
    pin, pout, zs, zr, as_, ar, ys, yr, ls, lr, xs, xr, bs, br, ss, sr, es, er,
    rxs, rxr, rls, rlr, rys, ryr, rzs, rzr,
):
    s, r = lax.axis_index("seq"), lax.axis_index("res")
    zh, c = lax.div(s, 2), lax.rem(s, 2)
    y, x, zl = lax.div(r, 8), lax.rem(lax.div(r, 2), 4), lax.rem(r, 2)
    role = mod4(y - zh)
    jb = x * 2 + zl

    def device(zh_, c_, y_, x_, zl_):
        return (zh_ * 2 + c_, y_ * 8 + x_ * 2 + zl_)

    def to_z(d):
        return device(mod4(zh + d), c, y, x, zl)

    def to_y(d):
        return device(zh, c, mod4(y + d), x, zl)

    def to_x(d):
        return device(zh, c, y, mod4(x + d), zl)

    dev_zl = device(zh, c, y, x, 1 - zl)
    dev_core = device(zh, 1 - c, y, x, zl)

    def remote(src, dst, ssem, rsem, dev):
        return pltpu.make_async_remote_copy(
            src_ref=src, dst_ref=dst, send_sem=ssem, recv_sem=rsem,
            device_id=dev, device_id_type=MESH,
        )

    def pair_copy(g):
        rows = pl.ds(16 * g, 16)
        return pltpu.make_async_copy(pair_in.at[rows], pair.at[rows], pin.at[g])

    def couple_copy(g):
        rows = pl.ds(16 * g, 16)
        return pltpu.make_async_copy(pair.at[rows], couple.at[rows], pout.at[g])

    def seq_of(u):
        return 2 * mod4(zh - gray(lax.div(u, 2))) + lax.rem(u, 2)

    def z_copy(src, dst, ssem, rsem, d, owner):
        return remote(src, dst.at[pl.ds(2 * owner, 2)], ssem.at[d - 1], rsem.at[d - 1], to_z(d))

    def y_copy(u, d):
        src = feat.at[u] if u < 2 else qf.at[seq_of(u)]
        return remote(src, kv.at[seq_of(u), jb], ys.at[u, d - 1], yr.at[u], to_y(d))

    def l_copy(u, b):
        here = kv.at[seq_of(u), b]
        return remote(here, here, ls.at[u], lr.at[u], dev_zl)

    def x_copy(u, d, owner):
        here = kv.at[seq_of(u), pl.ds(2 * owner, 2)]
        return remote(here, here, xs.at[u, d - 1], xr.at[u, d - 1], to_x(d))

    def stage_y(u):
        if u >= 2 and u % 2 == 0:
            d = (0, 1, 3, 2)[u // 2]
            z_copy(feat, qf, zs, zr, d, mod4(zh - d)).wait_recv()

        @pl.when(role == 0)
        def _():
            for d in (1, 3, 2):
                y_copy(u, d).start()
            kv[seq_of(u), jb] = feat[u] if u < 2 else qf[seq_of(u)]

    def stage_l(u):
        @pl.when(role != 0)
        def _():
            remote(
                kv.at[seq_of(u), jb], kv.at[seq_of(u), jb], ys.at[u, 0], yr.at[u], to_y(1)
            ).wait_recv()

        l_copy(u, jb).start()

    def stage_x(u):
        l_copy(u, 2 * x + 1 - zl).wait_recv()
        for d in (1, 3, 2):
            x_copy(u, d, x).start()

    def stage_w(u):
        for d in (1, 3, 2):
            x_copy(u, d, mod4(x - d)).wait_recv()

    for g in range(4):
        pair_copy(g).start()
    qf[pl.ds(2 * zh, 2)] = feat[...]
    ag[pl.ds(2 * zh, 2)] = adj[...]

    with scope("barrier"):
        barrier = pltpu.get_barrier_semaphore()
        partners = [to_z(d) for d in (1, 2, 3)] + [to_y(d) for d in (1, 2, 3)]
        partners += [to_x(d) for d in (1, 2, 3)] + [dev_zl, dev_core]
        for dev in partners:
            pl.semaphore_signal(barrier, inc=1, device_id=dev, device_id_type=MESH)
        pl.semaphore_wait(barrier, len(partners))

    stage_y(0)
    stage_y(1)
    for d in (1, 3, 2):
        z_copy(feat, qf, zs, zr, d, zh).start()
    for d in (1, 3, 2):
        z_copy(adj, ag, as_, ar, d, zh).start()

    row = lax.broadcasted_iota(jnp.int32, (128, 8), 0)
    col = lax.broadcasted_iota(jnp.int32, (128, 8), 1)
    rep = dot(jnp.where(lax.div(row, 16) == col, 1.0, 0.0).astype(BF16), wch[...], NT)
    spread_map(rep, wexp)

    def bias_group(g):
        pair_copy(g).wait()
        total = jnp.zeros((128, 256), F32)
        for p in range(8):
            i = 16 * g + 2 * p
            both = jnp.concatenate([pair[i], pair[i + 1]], axis=1)
            total += dot(wexp[:, p * 256 : (p + 1) * 256], both, NT)
        for h in range(8):
            bias[c, h * 64 + 16 * g : h * 64 + 16 * g + 16, :] = total[h * 16 : h * 16 + 16]

    with scope("bias_a"):
        bias_group(0)
        bias_group(1)
    with scope("hops_a"):
        stage_l(0)
        stage_l(1)
        stage_y(2)
        stage_y(3)
    with scope("bias_b"):
        bias_group(2)
    with scope("hops_b"):
        stage_y(4)
        stage_y(5)
        stage_x(0)
        stage_x(1)
    with scope("bias_c"):
        bias_group(3)
        swap = remote(bias.at[c], bias.at[c], bs, br, dev_core)
        swap.start()
    with scope("hops_c"):
        stage_y(6)
        stage_y(7)
        stage_l(2)
        stage_l(3)
        for d in (1, 3, 2):
            z_copy(adj, ag, as_, ar, d, mod4(zh - d)).wait_recv()

    lanes = lax.broadcasted_iota(jnp.int32, (64, 256), 1)
    masks = [(lanes >= 32 * h) & (lanes < 32 * h + 32) for h in range(8)]

    def query_side(n, carry):
        rows = qf[n]
        q = (dot(rows, wq[...]) * SCALE).astype(BF16).astype(F32)
        gate = jax.nn.sigmoid(dot(rows, wg[...]) + bg[...])
        dg = dot(ag[n], wo[...], NT)
        da = (dg * gate).astype(BF16).astype(F32)
        fac[n] = dg * gate * (1.0 - gate)
        for h in range(8):
            qbd[n, h * 64 : h * 64 + 64, :] = jnp.where(masks[h], q, 0.0).astype(BF16)
            dabd[n, h * 64 : h * 64 + 64, :] = jnp.where(masks[h], da, 0.0).astype(BF16)
        return carry

    with scope("query_a"):
        lax.fori_loop(0, 4, query_side, 0)
    with scope("hops_d"):
        stage_x(2)
        stage_x(3)
        stage_l(4)
        stage_l(5)
    with scope("query_b"):
        lax.fori_loop(4, 8, query_side, 0)
        remote(bias.at[1 - c], bias.at[1 - c], bs, br, dev_core).wait_recv()

    lane = lax.broadcasted_iota(jnp.int32, (64, 128), 1)

    def stat_copy(n, d):
        return remote(stout.at[n], stin.at[n, d - 1], ss.at[n, d - 1], sr.at[n, d - 1], to_z(d))

    def first(u, carry):
        n = seq_of(u)
        with scope("arrive"):
            stage_w(u)
        with scope("first"):
            rows = kv[n].reshape(512, 256)
            kbuf[n] = dot(rows, wk[...]).astype(BF16)
            vbuf[n] = dot(rows, wv[...]).astype(BF16)
            sbuf[...] = dot(qbd[n], kbuf[n], NT)
            dpbuf[n] = dot(dabd[n], vbuf[n], NT)
            tiles = []
            for h in range(8):
                rows = pl.ds(h * 64, 64)
                s0 = sbuf[rows, 0:256] + bias[0, rows, :]
                s1 = sbuf[rows, 256:512] + bias[1, rows, :]
                top = jnp.max(jnp.maximum(s0, s1), axis=1, keepdims=True)
                p0, p1 = jnp.exp(s0 - top), jnp.exp(s1 - top)
                pbuf[n, rows, 0:256] = p0
                pbuf[n, rows, 256:512] = p1
                total = jnp.sum(p0 + p1, axis=1, keepdims=True)
                mixed = jnp.sum(
                    p0 * dpbuf[n, rows, 0:256] + p1 * dpbuf[n, rows, 256:512],
                    axis=1, keepdims=True,
                )
                tiles.append(jnp.where(lane == 0, top, jnp.where(lane == 1, total, mixed)))
            stout[n] = jnp.concatenate(tiles, axis=0).T[0:8]
            for d in (1, 2, 3):
                stat_copy(n, d).start()

        @pl.when(u < 4)
        def _():
            stage_x(u + 4)

        @pl.when(u < 2)
        def _():
            stage_l(u + 6)

        return carry

    lax.fori_loop(0, 8, first, 0)

    def back_seq(u):
        return 2 * mod4(zh - gray(lax.rem(lax.div(u, 2) + 1, 4))) + lax.rem(u, 2)

    def rx_copy(u, d):
        return remote(
            part.at[u, pl.ds(2 * mod4(x + d), 2)], in_x.at[u, d - 1],
            rxs.at[u, d - 1], rxr.at[u, d - 1], to_x(d),
        )

    def rl_copy(u):
        return remote(hopl.at[u], in_l.at[u], rls.at[u], rlr.at[u], dev_zl)

    def ry_copy(u, k):
        return remote(hopy.at[u], in_y.at[u, k - 1], rys.at[u], ryr.at[u, k - 1], to_y(4 - k))

    def rz_copy(u):
        d = gray(lax.rem(lax.div(u, 2) + 1, 4))
        return remote(zout.at[u], zin.at[u], rzs.at[u], rzr.at[u], to_z(4 - d))

    def back_x(u):
        for d in (1, 3, 2):
            rx_copy(u, d).start()

    def back_l(u):
        for d in (1, 3, 2):
            rx_copy(u, d).wait_recv()

        def total(b):
            return (
                (part[u, 2 * x + b].astype(F32) + in_x[u, 0, b].astype(F32))
                + (in_x[u, 1, b].astype(F32) + in_x[u, 2, b].astype(F32))
            )

        acc[u] = total(zl)
        hopl[u] = total(1 - zl).astype(BF16)
        rl_copy(u).start()

    def back_y(u):
        rl_copy(u).wait_recv()
        acc[u] = acc[u] + in_l[u].astype(F32)
        for k in (1, 2, 3):

            @pl.when(role == k)
            def _():
                hopy[u] = acc[u].astype(BF16)
                ry_copy(u, k).start()

    def back_z(u):
        mine = ipart[u]

        @pl.when(role == 0)
        def _():
            for k in (1, 2, 3):
                ry_copy(u, k).wait_recv()
            acc[u] = (mine + acc[u] + in_y[u, 0].astype(F32)) + (
                in_y[u, 1].astype(F32) + in_y[u, 2].astype(F32)
            )

        @pl.when(role != 0)
        def _():
            acc[u] = mine

        @pl.when(u < 6)
        def _():
            zout[u] = acc[u].astype(BF16)
            rz_copy(u).start()

    dbias[...] = jnp.zeros_like(dbias)

    def second(u, carry):
        n = back_seq(u)
        with scope("stats"):
            for d in (1, 2, 3):
                stat_copy(n, d).wait_recv()
            tops = [stout[n, 0:1]] + [stin[n, d, 0:1] for d in range(3)]
            top = jnp.maximum(jnp.maximum(tops[0], tops[1]), jnp.maximum(tops[2], tops[3]))
            own = jnp.exp(tops[0] - top)
            total, mixed = own * stout[n, 1:2], own * stout[n, 2:3]
            for d in range(3):
                weight = jnp.exp(tops[d + 1] - top)
                total += weight * stin[n, d, 1:2]
                mixed += weight * stin[n, d, 2:3]
            down = lax.broadcasted_iota(jnp.int32, (128, 512), 0)
            ab = jnp.where(down == 0, own / total, mixed / total).T
        with scope("second"):
            for h in range(8):
                rows = pl.ds(h * 64, 64)
                a = ab[h * 64 : h * 64 + 64, 0:1]
                delta = ab[h * 64 : h * 64 + 64, 1:2]
                for half in (0, 1):
                    cols = slice(half * 256, half * 256 + 256)
                    probs = pbuf[n, rows, cols] * a
                    pb[rows, cols] = probs.astype(BF16)
                    ds = probs * (dpbuf[n, rows, cols] - delta)
                    dsb[rows, cols] = ds.astype(BF16)
                    dbias[half, rows, :] += ds
            att_all = dot(pb[...], vbuf[n])
            dq_all = dot(dsb[...], kbuf[n])
            att, dq = jnp.zeros((64, 256), F32), jnp.zeros((64, 256), F32)
            for h in range(8):
                att += jnp.where(masks[h], att_all[h * 64 : h * 64 + 64], 0.0)
                dq += jnp.where(masks[h], dq_all[h * 64 : h * 64 + 64], 0.0)
            dq = (dq * SCALE).astype(BF16)
            dgp = (fac[n] * att).astype(BF16)
            ipart[u] = dot(dq, wq[...], NT) + dot(dgp, wg[...], NT)
            dk = dot(qbd[n], dsb[...], TN).T.astype(BF16)
            dv = dot(dabd[n], pb[...], TN).T.astype(BF16)
            part[u] = (
                (dot(dk, wk[...], NT) + dot(dv, wv[...], NT)).astype(BF16).reshape(8, 64, 256)
            )
        with scope("back"):
            back_x(u)

            @pl.when(u >= 3)
            def _():
                back_l(u - 3)

            @pl.when(u >= 5)
            def _():
                back_y(u - 5)

            @pl.when(u >= 7)
            def _():
                back_z(u - 7)

        return carry

    lax.fori_loop(0, 8, second, 0)

    def couple_group(g):
        rows = jnp.concatenate(
            [
                dbias[c, h * 64 + 16 * g : h * 64 + 16 * g + 16, :]
                + dbin[h * 64 + 16 * g : h * 64 + 16 * g + 16, :]
                for h in range(8)
            ],
            axis=0,
        )
        high = rows.astype(BF16)
        low = (rows - high.astype(F32)).astype(BF16)
        both = jnp.concatenate([high, low], axis=0).T
        for p in range(8):
            w = wexp[:, p * 256 : (p + 1) * 256]
            res = dot(both, jnp.concatenate([w, w], axis=0)).astype(BF16)
            pair[16 * g + 2 * p] = res[:, 0:128]
            pair[16 * g + 2 * p + 1] = res[:, 128:256]
        couple_copy(g).start()

    give = remote(dbias.at[1 - c], dbin, es, er, dev_core)
    give.start()
    with scope("tail_a"):
        back_l(5)
        back_y(3)
        back_z(1)
        back_y(4)
        give.wait_recv()
    with scope("couple_a"):
        couple_group(0)
    with scope("tail_b"):
        back_l(6)
        back_z(2)
        back_y(5)
        back_z(3)
    with scope("couple_b"):
        couple_group(1)
    with scope("tail_c"):
        back_l(7)
        back_z(4)
        back_y(6)
        back_z(5)
    with scope("couple_c"):
        couple_group(2)
    with scope("tail_d"):
        back_y(7)
    with scope("couple_d"):
        couple_group(3)
    with scope("tail_e"):
        back_z(6)
        back_z(7)
        for u in range(6):
            rz_copy(u).wait_recv()
        for e in (0, 1):
            out[e] = (
                (acc[6 + e] + zin[e].astype(F32))
                + (zin[2 + e].astype(F32) + zin[4 + e].astype(F32))
            ).astype(BF16)

    with scope("drain"):
        for d in (1, 3, 2):
            z_copy(feat, qf, zs, zr, d, zh).wait_send()
            z_copy(adj, ag, as_, ar, d, zh).wait_send()
        swap.wait_send()
        give.wait_send()

        @pl.when(role == 0)
        def _():
            for u in range(8):
                for d in (1, 3, 2):
                    y_copy(u, d).wait_send()

        @pl.when(role != 0)
        def _():
            for u in range(8):
                ry_copy(u, 1).wait_send()

        def drain(u, carry):
            l_copy(u, jb).wait_send()
            for d in (1, 3, 2):
                x_copy(u, d, x).wait_send()
                stat_copy(u, d).wait_send()
                rx_copy(u, d).wait_send()
            rl_copy(u).wait_send()

            @pl.when(u < 6)
            def _():
                rz_copy(u).wait_send()

            return carry

        lax.fori_loop(0, 8, drain, 0)
        for g in range(4):
            couple_copy(g).wait()


VM = pl.BlockSpec(memory_space=pltpu.VMEM)
HBM = pl.BlockSpec(memory_space=pl.ANY)
DMA = pltpu.SemaphoreType.DMA


def per_device(feat, pair, adj, wq, wk, wv, wg, bg, wch, wo):
    sds, vmem = jax.ShapeDtypeStruct, pltpu.VMEM
    return pl.pallas_call(
        kernel,
        out_shape=(sds((2, 64, 256), BF16), sds((64, 256, 128), BF16)),
        in_specs=[VM, HBM] + [VM] * 8,
        out_specs=(VM, HBM),
        scratch_shapes=[
            vmem((64, 256, 128), BF16),
            vmem((8, 64, 256), BF16),
            vmem((8, 64, 256), BF16),
            vmem((8, 8, 64, 256), BF16),
            vmem((2, 512, 256), F32),
            vmem((2, 512, 256), F32),
            vmem((512, 256), F32),
            vmem((8, 512, 512), F32),
            vmem((8, 512, 512), F32),
            vmem((8, 512, 256), BF16),
            vmem((8, 512, 256), BF16),
            vmem((8, 512, 256), BF16),
            vmem((8, 512, 256), BF16),
            vmem((8, 64, 256), F32),
            vmem((512, 512), F32),
            vmem((512, 512), BF16),
            vmem((512, 512), BF16),
            vmem((128, 2048), BF16),
            vmem((8, 8, 512), F32),
            vmem((8, 3, 8, 512), F32),
            vmem((8, 64, 256), F32),
            vmem((8, 8, 64, 256), BF16),
            vmem((8, 3, 2, 64, 256), BF16),
            vmem((8, 64, 256), F32),
            vmem((8, 64, 256), BF16),
            vmem((8, 64, 256), BF16),
            vmem((8, 64, 256), BF16),
            vmem((8, 3, 64, 256), BF16),
            vmem((6, 64, 256), BF16),
            vmem((6, 64, 256), BF16),
            DMA((4,)), DMA((4,)),
            DMA((3,)), DMA((3,)), DMA((3,)), DMA((3,)),
            DMA((8, 3)), DMA((8,)), DMA((8,)), DMA((8,)), DMA((8, 3)), DMA((8, 3)),
            DMA, DMA, DMA((8, 3)), DMA((8, 3)), DMA, DMA,
            DMA((8, 3)), DMA((8, 3)), DMA((8,)), DMA((8,)), DMA((8,)), DMA((8, 3)),
            DMA((6,)), DMA((6,)),
        ],
        compiler_params=pltpu.CompilerParams(
            collective_id=0, has_side_effects=True, vmem_limit_bytes=VMEM_LIMIT
        ),
        name="fused",
    )(feat, pair, adj, wq, wk, wv, wg, bg.reshape(1, 256), wch, wo)


def solution(mesh):
    in_specs = (
        P("seq", "res", None), P("res", "seq", None), P("seq", "res", None),
        P(), P(), P(), P(), P(), P(), P(),
    )
    out_specs = (P("seq", "res", None), P("res", "seq", None))
    return jax.shard_map(
        per_device, mesh=mesh, in_specs=in_specs, out_specs=out_specs, check_vma=False
    )
```

```python
import jax
import jax.numpy as jnp
from jax import lax
from jax.experimental import pallas as pl
from jax.experimental.pallas import tpu as pltpu
from jax.sharding import PartitionSpec as P

F32, BF16 = jnp.float32, jnp.bfloat16
MESH = pl.DeviceIdType.MESH
NT = (((1,), (1,)), ((), ()))
TN = (((0,), (0,)), ((), ()))
VMEM_LIMIT = 61 * 1024 * 1024
SCALE = 32**-0.5
LAGS = (3, 5)
SHIFT = 8


def dot(a, b, dims=(((1,), (0,)), ((), ()))):
    return lax.dot_general(a, b, dims, preferred_element_type=F32)


def mod4(v):
    return lax.rem(v + 8, 4)


def first_chunk(p, zh):
    later = lax.div(p + 3, 4)
    return (1 - later) * zh + later * (p - 1 + lax.div(p + 3 - zh, 4))


def second_chunk(p, zh):
    last = lax.div(p, 3)
    return last * zh + (1 - last) * (p + lax.div(p + 4 - zh, 4))


def differ(a, b):
    return lax.div((a - b) * (a - b) + 8, 9)


def spread_map(rep, out):
    row = lax.broadcasted_iota(jnp.int32, (128, 128), 0)
    for i in range(16):
        out[:, i * 128 : (i + 1) * 128] = jnp.where(lax.rem(row, 16) == i, rep, 0.0).astype(BF16)


def kernel(
    feat, pair_in, adj, wq_in, wk_in, wv_in, wg_in, bg, wch, wo_in,
    out, db,
    wq, wk, wv, wg, wo, pair, qf, ag, kv, bias, dbias, dbin, pbuf, dpbuf, kbuf, vbuf, qbd, dabd, fac,
    sbuf, pb, dsb, wexp, stout, stin, dbout, ebuf, ipart, part, in_x, hop, in_y, acc, tout, tin, zout, zin,
    win, pin, pout, zs, zr, as_, ar, vs, vr, ys, yr, xs, xr, bs, br, ss, sr, es, er,
    rxs, rxr, rys, ryr, rts, rtr, rzs, rzr,
):
    s, r = lax.axis_index("seq"), lax.axis_index("res")
    zh, c = lax.div(s, 2), lax.rem(s, 2)
    y, x, zl = lax.div(r, 8), lax.rem(lax.div(r, 2), 4), lax.rem(r, 2)
    off_a = differ(y, zh)
    off_b = lax.div(differ(x, y) + differ(y, zh) + 1, 2)

    def wide_at(e):
        return (1 - e) * x + e * y

    def thin_at(e):
        return (1 - e) * y + e * x

    def device(zh_, c_, y_, x_, zl_):
        return (zh_ * 2 + c_, y_ * 8 + x_ * 2 + zl_)

    def to_z(d):
        return device(mod4(zh + d), c, y, x, zl)

    def to_y(d):
        return device(zh, c, mod4(y + d), x, zl)

    def to_x(d):
        return device(zh, c, y, mod4(x + d), zl)

    dev_zl = device(zh, c, y, x, 1 - zl)
    dev_core = device(zh, 1 - c, y, x, zl)

    def remote(src, dst, ssem, rsem, dev):
        return pltpu.make_async_remote_copy(
            src_ref=src, dst_ref=dst, send_sem=ssem, recv_sem=rsem,
            device_id=dev, device_id_type=MESH,
        )

    def pair_copy(g):
        rows = pl.ds(16 * g, 16)
        return pltpu.make_async_copy(pair_in.at[rows], pair.at[rows], pin.at[g])

    def weight_copy(k):
        src, dst = ((wch, None), (wq_in, wq), (wg_in, wg), (wo_in, wo), (wk_in, wk), (wv_in, wv))[k]
        return pltpu.make_async_copy(src, dst, win.at[k - 1])

    def seq_of(u):
        return 2 * first_chunk(lax.div(u, 2), zh) + lax.rem(u, 2)

    def z_copy(src, dst, ssem, rsem, d, owner):
        return remote(src, dst.at[pl.ds(2 * owner, 2)], ssem.at[d - 1], rsem.at[d - 1], to_z(d))

    dev_swapped = device(y, c, zh, x, zl)
    dev_next, dev_previous = device(y, c, x, zh, zl), device(x, c, zh, y, zl)

    def wide_to(e, d):
        xx, yy = (1 - e) * mod4(x + d) + e * x, e * mod4(y + d) + (1 - e) * y
        return device(zh, c, yy, xx, zl)

    def thin_to(e, k, cross):
        return device(zh, c, (1 - e) * k + e * y, e * k + (1 - e) * x, lax.rem(zl + cross, 2))

    def e_copy(e):
        return remote(
            feat.at[e], ebuf.at[e], vs.at[e], vr.at[e], (dev_swapped, dev_next)[e]
        )

    def y_copy(src, e, d, cross):
        k = thin_at(e)
        here = kv.at[2 * k + e, 2 * wide_at(e) + zl]
        return remote(
            src, here, ys.at[e, d, cross], yr.at[2 * k + e, cross], thin_to(e, mod4(k + d), cross)
        )

    Y_ALL = [(d, cross) for d in (1, 3, 2, 0) for cross in (0, 1) if d or cross]

    def stage_y(src, e):
        for d, cross in Y_ALL:
            y_copy(src, e, d, cross).start()
        kv[2 * thin_at(e) + e, 2 * wide_at(e) + zl] = src[...]

    def y_arrived(u):
        n, e = seq_of(u), lax.rem(u, 2)

        def wait(cross, b):
            here = kv.at[n, b]
            remote(here, here, ys.at[0, 0, cross], yr.at[n, cross], dev_zl).wait_recv()

        pl.when(thin_at(e) != first_chunk(lax.div(u, 2), zh))(
            lambda: wait(0, 2 * wide_at(e) + zl)
        )
        wait(1, 2 * wide_at(e) + 1 - zl)

    def x_copy(u, d, owner):
        here = kv.at[seq_of(u), pl.ds(2 * owner, 2)]
        return remote(here, here, xs.at[u, d - 1], xr.at[u, d - 1], wide_to(lax.rem(u, 2), d))

    def stage_x(u):
        for d in (1, 3, 2):
            x_copy(u, d, wide_at(lax.rem(u, 2))).start()

    def stage_w(u):
        for d in (1, 3, 2):
            x_copy(u, d, mod4(wide_at(lax.rem(u, 2)) - d)).wait_recv()

    barrier = pltpu.get_barrier_semaphore()
    partners = [to_z(d) for d in (1, 2, 3)] + [to_y(d) for d in (1, 2, 3)]
    partners += [device(zh, c, mod4(y + d), x, 1 - zl) for d in (0, 1, 2, 3)]
    partners += [device(zh, c, y, mod4(x + d), 1 - zl) for d in (1, 2, 3)]
    partners += [to_x(d) for d in (1, 2, 3)] + [dev_core]
    for dev in partners:
        pl.semaphore_signal(barrier, inc=1, device_id=dev, device_id_type=MESH)

    @pl.when(off_a != 0)
    def _():
        pl.semaphore_signal(barrier, inc=1, device_id=dev_swapped, device_id_type=MESH)

    @pl.when(off_b != 0)
    def _():
        pl.semaphore_signal(barrier, inc=1, device_id=dev_next, device_id_type=MESH)
        pl.semaphore_signal(barrier, inc=1, device_id=dev_previous, device_id_type=MESH)

    for g in range(4):
        pair_copy(g).start()
    for k in range(1, 6):
        weight_copy(k).start()
    qf[pl.ds(2 * zh, 2)] = feat[...]
    ag[pl.ds(2 * zh, 2)] = adj[...]
    row = lax.broadcasted_iota(jnp.int32, (128, 8), 0)
    col = lax.broadcasted_iota(jnp.int32, (128, 8), 1)
    rep = dot(jnp.where(lax.div(row, 16) == col, 1.0, 0.0).astype(BF16), wch[...])
    spread_map(rep, wexp)
    dbias[...] = jnp.zeros_like(dbias)
    pl.semaphore_wait(barrier, len(partners) + off_a + 2 * off_b)

    @pl.when(off_a == 0)
    def _():
        stage_y(feat.at[0], 0)

    @pl.when(off_a != 0)
    def _():
        e_copy(0).start()

    @pl.when(off_b == 0)
    def _():
        stage_y(feat.at[1], 1)

    @pl.when(off_b != 0)
    def _():
        e_copy(1).start()

    for d in (1, 3, 2):
        z_copy(feat, qf, zs, zr, d, zh).start()

    def bias_group(g):
        pair_copy(g).wait()
        total = jnp.zeros((128, 256), F32)
        for p in range(8):
            i = 16 * g + 2 * p
            both = jnp.concatenate([pair[i], pair[i + 1]], axis=1)
            total += dot(wexp[:, p * 256 : (p + 1) * 256], both, NT)
        for h in range(8):
            bias[c, h * 64 + 16 * g : h * 64 + 16 * g + 16, :] = total[h * 16 : h * 16 + 16]

    bias_group(0)
    bias_group(1)
    bias_group(2)
    y_arrived(0)
    stage_x(0)

    @pl.when(off_b != 0)
    def _():
        e_copy(1).wait_recv()
        stage_y(ebuf.at[1], 1)

    @pl.when(off_a != 0)
    def _():
        e_copy(0).wait_recv()
        stage_y(ebuf.at[0], 0)

    for d in (1, 3, 2):
        z_copy(adj, ag, as_, ar, d, zh).start()
    bias_group(3)
    swap = remote(bias.at[c], bias.at[c], bs, br, dev_core)
    swap.start()
    for k in range(1, 6):
        weight_copy(k).wait()

    lanes = lax.broadcasted_iota(jnp.int32, (64, 256), 1)
    masks = [(lanes >= 32 * h) & (lanes < 32 * h + 32) for h in range(8)]

    def query_side(n):
        rows = qf[n]
        q = (dot(rows, wq[...]) * SCALE).astype(BF16).astype(F32)
        gate = jax.nn.sigmoid(dot(rows, wg[...]) + bg[...])
        dg = dot(ag[n], wo[...], NT)
        da = (dg * gate).astype(BF16).astype(F32)
        fac[n] = dg * gate * (1.0 - gate)
        for h in range(8):
            qbd[n, h * 64 : h * 64 + 64, :] = jnp.where(masks[h], q, 0.0).astype(BF16)
            dabd[n, h * 64 : h * 64 + 64, :] = jnp.where(masks[h], da, 0.0).astype(BF16)

    query_side(seq_of(0))
    query_side(seq_of(1))
    y_arrived(1)
    stage_x(1)
    y_arrived(2)
    stage_x(2)
    y_arrived(3)
    stage_x(3)
    remote(bias.at[1 - c], bias.at[1 - c], bs, br, dev_core).wait_recv()

    lane = lax.broadcasted_iota(jnp.int32, (64, 128), 1)

    def stat_copy(n, d):
        return remote(stout.at[n], stin.at[n, d - 1], ss.at[n, d - 1], sr.at[n, d - 1], to_z(d))

    def first(u):
        n = seq_of(u)
        @pl.when((u >= 2) & (lax.rem(u, 2) == 0))
        def _():
            owner = first_chunk(lax.div(u, 2), zh)
            z_copy(feat, qf, zs, zr, mod4(zh - owner), owner).wait_recv()
            z_copy(adj, ag, as_, ar, mod4(zh - owner), owner).wait_recv()

        @pl.when(u >= 2)
        def _():
            query_side(n)

        stage_w(u)
        rows = kv[n].reshape(512, 256)
        kbuf[n] = dot(rows, wk[...]).astype(BF16)
        vbuf[n] = dot(rows, wv[...]).astype(BF16)
        sbuf[...] = dot(qbd[n], kbuf[n], NT)
        dpbuf[n] = dot(dabd[n], vbuf[n], NT)
        tiles = []
        for h in range(8):
            rows = pl.ds(h * 64, 64)
            s0 = sbuf[rows, 0:256] + bias[0, rows, :]
            s1 = sbuf[rows, 256:512] + bias[1, rows, :]
            top = jnp.max(jnp.maximum(s0, s1), axis=1, keepdims=True)
            p0, p1 = jnp.exp(s0 - top), jnp.exp(s1 - top)
            pbuf[n, rows, 0:256] = p0
            pbuf[n, rows, 256:512] = p1
            total = jnp.sum(p0 + p1, axis=1, keepdims=True)
            mixed = jnp.sum(
                p0 * dpbuf[n, rows, 0:256] + p1 * dpbuf[n, rows, 256:512], axis=1, keepdims=True
            )
            tiles.append(jnp.where(lane == 0, top, jnp.where(lane == 1, total, mixed)))
        stats = jnp.concatenate(tiles, axis=0).T[0:4]
        for k in range(4):
            stout[n, 4 * k : 4 * k + 4, :] = stats[:, 128 * k : 128 * k + 128]
        for d in (1, 3, 2):
            stat_copy(n, d).start()

        @pl.when(u < 4)
        def _():
            y_arrived(u + 4)
            stage_x(u + 4)

    def odd(u):
        return 1 - lax.rem(u, 2)

    def back_seq(u):
        return 2 * second_chunk(lax.div(u, 2), zh) + odd(u)

    def rx_copy(u, d):
        e = odd(u)
        return remote(
            part.at[u, pl.ds(2 * mod4(wide_at(e) + d), 2)], in_x.at[u, d - 1],
            rxs.at[u, d - 1], rxr.at[u, d - 1], wide_to(e, d),
        )

    def ry_copy(u, cross):
        e, k = odd(u), second_chunk(lax.div(u, 2), zh)
        slot = 2 * mod4(thin_at(e) - k) + cross
        return remote(
            hop.at[u, cross], in_y.at[e, slot], rys.at[u, cross], ryr.at[e, slot],
            thin_to(e, k, cross),
        )

    def ry_arrived(e, slot):
        remote(hop.at[0, 0], in_y.at[e, slot], rys.at[0, 0], ryr.at[e, slot], dev_zl).wait_recv()

    def rt_copy(e):
        return remote(
            tout.at[e], tin.at[e], rts.at[e], rtr.at[e], (dev_swapped, dev_previous)[e]
        )

    def rz_copy(u):
        owner = second_chunk(lax.div(u, 2), zh)
        slot = 2 * (mod4(owner - zh) - 1) + odd(u)
        return remote(
            zout.at[u], zin.at[slot], rzs.at[u], rzr.at[slot], device(owner, c, y, x, zl)
        )

    def rz_arrived(slot):
        remote(zout.at[slot], zin.at[slot], rzs.at[slot], rzr.at[slot], to_z(1)).wait_recv()

    def back_x(u):
        for d in (1, 3, 2):
            rx_copy(u, d).start()

    def x_total(u, b):
        mine = part[u, 2 * wide_at(odd(u)) + b]
        return (mine.astype(F32) + in_x[u, 0, b].astype(F32)) + (
            in_x[u, 1, b].astype(F32) + in_x[u, 2, b].astype(F32)
        )

    def back_y(u):
        for d in (1, 3, 2):
            rx_copy(u, d).wait_recv()
        hop[u, 1] = x_total(u, 1 - zl).astype(BF16)
        ry_copy(u, 1).start()
        own = x_total(u, zl)
        away = thin_at(odd(u)) != second_chunk(lax.div(u, 2), zh)

        @pl.when(away)
        def _():
            hop[u, 0] = own.astype(BF16)
            ry_copy(u, 0).start()

        @pl.when(jnp.logical_not(away))
        def _():
            acc[odd(u)] = own

    def back_t(u):
        def finish(e):
            for slot in range(1, 8):
                ry_arrived(e, slot)
            got = [in_y[e, slot].astype(F32) for slot in range(1, 8)]
            total = ((acc[e] + got[0]) + (got[1] + got[2])) + ((got[3] + got[4]) + (got[5] + got[6]))
            acc[e] = total

            @pl.when((off_a, off_b)[e] != 0)
            def _():
                tout[e] = total.astype(BF16)
                rt_copy(e).start()

        k = second_chunk(lax.div(u, 2), zh)
        for e in (0, 1):
            pl.when((odd(u) == e) & (thin_at(e) == k))(lambda: finish(e))

    def second(u):
        n = back_seq(u)
        for d in (1, 3, 2):
            stat_copy(n, d).wait_recv()

        def wide(v):
            return jnp.concatenate([v[4 * k : 4 * k + 4] for k in range(4)], axis=1)

        own_stats = wide(stout[n])
        others = [wide(stin[n, d]) for d in range(3)]
        tops = [own_stats[0:1]] + [o[0:1] for o in others]
        top = jnp.maximum(jnp.maximum(tops[0], tops[1]), jnp.maximum(tops[2], tops[3]))
        own = jnp.exp(tops[0] - top)
        total, mixed = own * own_stats[1:2], own * own_stats[2:3]
        for d in range(3):
            weight = jnp.exp(tops[d + 1] - top)
            total += weight * others[d][1:2]
            mixed += weight * others[d][2:3]
        down = lax.broadcasted_iota(jnp.int32, (128, 512), 0)
        ab = jnp.where(down == 0, own / total, mixed / total).T
        for h in range(8):
            rows = pl.ds(h * 64, 64)
            a = ab[h * 64 : h * 64 + 64, 0:1]
            delta = ab[h * 64 : h * 64 + 64, 1:2]
            for half in (0, 1):
                cols = slice(half * 256, half * 256 + 256)
                probs = pbuf[n, rows, cols] * a
                pb[rows, cols] = probs.astype(BF16)
                ds = probs * (dpbuf[n, rows, cols] - delta)
                dsb[rows, cols] = ds.astype(BF16)
                dbias[half, rows, :] += ds
        att_all = dot(pb[...], vbuf[n])
        dq_all = dot(dsb[...], kbuf[n])
        att, dq = jnp.zeros((64, 256), F32), jnp.zeros((64, 256), F32)
        for h in range(8):
            att += jnp.where(masks[h], att_all[h * 64 : h * 64 + 64], 0.0)
            dq += jnp.where(masks[h], dq_all[h * 64 : h * 64 + 64], 0.0)
        dq = (dq * SCALE).astype(BF16)
        dgp = (fac[n] * att).astype(BF16)
        ipart[u] = dot(dq, wq[...], NT) + dot(dgp, wg[...], NT)

        @pl.when(u < 6)
        def _():
            zout[u] = ipart[u].astype(BF16)
            rz_copy(u).start()

        dk = dot(qbd[n], dsb[...], TN).T.astype(BF16)
        dv = dot(dabd[n], pb[...], TN).T.astype(BF16)
        part[u] = (
            (dot(dk, wk[...], NT) + dot(dv, wv[...], NT)).astype(BF16).reshape(8, 64, 256)
        )
        back_x(u)

    LY, LT = LAGS

    def step(t, carry):
        @pl.when(t < 8)
        def _():
            first(t)

        @pl.when(t >= SHIFT)
        def _():
            second(t - SHIFT)

        for lag, stage in ((LY, back_y), (LT, back_t)):
            if lag < 8:
                pl.when(t >= SHIFT + lag)(lambda: stage(t - SHIFT - lag))

        return carry

    lax.fori_loop(0, 8 + SHIFT, step, 0)
    give = remote(dbias.at[1 - c], dbin, es, er, dev_core)
    give.start()
    waits = [(back_y, u, u + LY) for u in range(8)] + [(back_t, u, u + LT) for u in range(8)]
    for fun, u, when in sorted((w for w in waits if w[2] > 7), key=lambda w: w[2]):
        fun(u)
    give.wait_recv()
    dbout[...] = dbias[c] + dbin[...]
    db_copy = pltpu.make_async_copy(dbout, db, pout)
    db_copy.start()
    for u in range(6):
        rz_arrived(u)

    for e in (0, 1):

        @pl.when((off_a, off_b)[e] != 0)
        def _():
            rt_copy(e).wait_recv()
            acc[e] = tin[e].astype(F32)

    for e in (0, 1):
        out[e] = (
            (acc[e] + ipart[7 - e] + zin[e].astype(F32))
            + (zin[2 + e].astype(F32) + zin[4 + e].astype(F32))
        ).astype(BF16)

    for d in (1, 3, 2):
        z_copy(feat, qf, zs, zr, d, zh).wait_send()
        z_copy(adj, ag, as_, ar, d, zh).wait_send()
    swap.wait_send()
    give.wait_send()

    for e in (0, 1):
        for d, cross in Y_ALL:
            y_copy(feat.at[e], e, d, cross).wait_send()

        @pl.when((off_a, off_b)[e] != 0)
        def _():
            e_copy(e).wait_send()
            rt_copy(e).wait_send()

    def drain(u, carry):
        for d in (1, 3, 2):
            x_copy(u, d, wide_at(lax.rem(u, 2))).wait_send()
            stat_copy(u, d).wait_send()
            rx_copy(u, d).wait_send()
        ry_copy(u, 1).wait_send()

        @pl.when(thin_at(odd(u)) != second_chunk(lax.div(u, 2), zh))
        def _():
            ry_copy(u, 0).wait_send()

        @pl.when(u < 6)
        def _():
            rz_copy(u).wait_send()

        return carry

    lax.fori_loop(0, 8, drain, 0)
    db_copy.wait()


def couple_kernel(db, wch, hom, couple, out, wide, store, sems):
    row = lax.broadcasted_iota(jnp.int32, (128, 8), 0)
    col = lax.broadcasted_iota(jnp.int32, (128, 8), 1)
    rep = dot(jnp.where(lax.div(row, 16) == col, 1.0, 0.0).astype(BF16), wch[...])
    spread_map(rep, wide)
    out[...] = hom[...]

    def copy(g):
        rows = pl.ds(16 * g, 16)
        return pltpu.make_async_copy(store.at[rows], couple.at[rows], sems.at[g])

    for g in range(4):
        rows = jnp.concatenate(
            [db[h * 64 + 16 * g : h * 64 + 16 * g + 16, :] for h in range(8)], axis=0
        )
        high = rows.astype(BF16)
        low = (rows - high.astype(F32)).astype(BF16)
        both = jnp.concatenate([high, low], axis=0).T
        for p in range(8):
            w = wide[:, p * 256 : (p + 1) * 256]
            res = dot(both, jnp.concatenate([w, w], axis=0)).astype(BF16)
            store[16 * g + 2 * p] = res[:, 0:128]
            store[16 * g + 2 * p + 1] = res[:, 128:256]
        copy(g).start()
    for g in range(4):
        copy(g).wait()


VM = pl.BlockSpec(memory_space=pltpu.VMEM)
HBM = pl.BlockSpec(memory_space=pl.ANY)
DMA = pltpu.SemaphoreType.DMA


def per_device(feat, pair, adj, wq, wk, wv, wg, bg, wch, wo):
    sds, vmem = jax.ShapeDtypeStruct, pltpu.VMEM
    wch = wch.T
    hom, db = pl.pallas_call(
        kernel,
        out_shape=(sds((2, 64, 256), BF16), sds((512, 256), F32)),
        in_specs=[VM, HBM, VM, HBM, HBM, HBM, HBM, VM, VM, HBM],
        out_specs=(VM, HBM),
        scratch_shapes=[vmem((256, 256), BF16)] * 5
        + [
            vmem((64, 256, 128), BF16),
            vmem((8, 64, 256), BF16),
            vmem((8, 64, 256), BF16),
            vmem((8, 8, 64, 256), BF16),
            vmem((2, 512, 256), F32),
            vmem((2, 512, 256), F32),
            vmem((512, 256), F32),
            vmem((8, 512, 512), F32),
            vmem((8, 512, 512), F32),
            vmem((8, 512, 256), BF16),
            vmem((8, 512, 256), BF16),
            vmem((8, 512, 256), BF16),
            vmem((8, 512, 256), BF16),
            vmem((8, 64, 256), F32),
            vmem((512, 512), F32),
            vmem((512, 512), BF16),
            vmem((512, 512), BF16),
            vmem((128, 2048), BF16),
            vmem((8, 16, 128), F32),
            vmem((8, 3, 16, 128), F32),
            vmem((512, 256), F32),
            vmem((2, 64, 256), BF16),
            vmem((8, 64, 256), F32),
            vmem((8, 8, 64, 256), BF16),
            vmem((8, 3, 2, 64, 256), BF16),
            vmem((8, 2, 64, 256), BF16),
            vmem((2, 8, 64, 256), BF16),
            vmem((2, 64, 256), F32),
            vmem((2, 64, 256), BF16),
            vmem((2, 64, 256), BF16),
            vmem((6, 64, 256), BF16),
            vmem((6, 64, 256), BF16),
            DMA((5,)), DMA((4,)), DMA,
            DMA((3,)), DMA((3,)), DMA((3,)), DMA((3,)),
            DMA((2,)), DMA((2,)), DMA((2, 4, 2)), DMA((8, 2)), DMA((8, 3)), DMA((8, 3)),
            DMA, DMA, DMA((8, 3)), DMA((8, 3)), DMA, DMA,
            DMA((8, 3)), DMA((8, 3)), DMA((8, 2)), DMA((2, 8)), DMA((2,)), DMA((2,)),
            DMA((6,)), DMA((6,)),
        ],
        compiler_params=pltpu.CompilerParams(
            collective_id=0, has_side_effects=True, vmem_limit_bytes=VMEM_LIMIT
        ),
        name="fused",
    )(feat, pair, adj, wq, wk, wv, wg, bg.reshape(1, 256), wch, wo)
    couple, homolog = pl.pallas_call(
        couple_kernel,
        out_shape=(sds((64, 256, 128), BF16), sds((2, 64, 256), BF16)),
        in_specs=[VM] * 3,
        out_specs=(HBM, VM),
        scratch_shapes=[vmem((128, 2048), BF16), vmem((64, 256, 128), BF16), DMA((4,))],
        compiler_params=pltpu.CompilerParams(vmem_limit_bytes=VMEM_LIMIT),
        name="couple",
    )(db, wch, hom)
    return homolog, couple


def solution(mesh):
    in_specs = (
        P("seq", "res", None), P("res", "seq", None), P("seq", "res", None),
        P(), P(), P(), P(), P(), P(), P(),
    )
    out_specs = (P("seq", "res", None), P("res", "seq", None))
    return jax.shard_map(
        per_device, mesh=mesh, in_specs=in_specs, out_specs=out_specs, check_vma=False
    )
```

```python
import jax
import jax.numpy as jnp
from jax import lax
from jax.experimental import pallas as pl
from jax.experimental.pallas import tpu as pltpu
from jax.sharding import PartitionSpec as P

F32, BF16 = jnp.float32, jnp.bfloat16
MESH = pl.DeviceIdType.MESH
NT = (((1,), (1,)), ((), ()))
TN = (((0,), (0,)), ((), ()))
VMEM_LIMIT = 61 * 1024 * 1024
SCALE = 32**-0.5
LAGS = (3, 5)
SHIFT = 8


def dot(a, b, dims=(((1,), (0,)), ((), ()))):
    return lax.dot_general(a, b, dims, preferred_element_type=F32)


def mod4(v):
    return lax.rem(v + 8, 4)


def first_chunk(p, zh):
    later = lax.div(p + 3, 4)
    return (1 - later) * zh + later * (p - 1 + lax.div(p + 3 - zh, 4))


def second_chunk(p, zh):
    last = lax.div(p, 3)
    return last * zh + (1 - last) * (p + lax.div(p + 4 - zh, 4))


def differ(a, b):
    return lax.div((a - b) * (a - b) + 8, 9)


def spread_map(rep, out):
    row = lax.broadcasted_iota(jnp.int32, (128, 128), 0)
    for i in range(16):
        out[:, i * 128 : (i + 1) * 128] = jnp.where(lax.rem(row, 16) == i, rep, 0.0).astype(BF16)


def kernel(
    feat, pair_in, adj, wq_in, wk_in, wv_in, wg_in, bg, wch, wo_in,
    out, db,
    wq, wk, wv, wg, wo, pair, qf, ag, kv, bias, dbias, dbin, pbuf, dpbuf, kbuf, vbuf, qbd, dabd, fac,
    sbuf, cw, sp, wexp, stout, stin, dbout, ebuf, ipart, part, in_x, hop, in_y, acc, tout, tin, zout, zin,
    win, pin, pout, zs, zr, as_, ar, vs, vr, ys, yr, xs, xr, bs, br, ss, sr, es, er,
    rxs, rxr, rys, ryr, rts, rtr, rzs, rzr,
):
    s, r = lax.axis_index("seq"), lax.axis_index("res")
    zh, c = lax.div(s, 2), lax.rem(s, 2)
    y, x, zl = lax.div(r, 8), lax.rem(lax.div(r, 2), 4), lax.rem(r, 2)
    off_a = differ(y, zh)
    off_b = lax.div(differ(x, y) + differ(y, zh) + 1, 2)

    def wide_at(e):
        return (1 - e) * x + e * y

    def thin_at(e):
        return (1 - e) * y + e * x

    def device(zh_, c_, y_, x_, zl_):
        return (zh_ * 2 + c_, y_ * 8 + x_ * 2 + zl_)

    def to_z(d):
        return device(mod4(zh + d), c, y, x, zl)

    def to_y(d):
        return device(zh, c, mod4(y + d), x, zl)

    def to_x(d):
        return device(zh, c, y, mod4(x + d), zl)

    dev_zl = device(zh, c, y, x, 1 - zl)
    dev_core = device(zh, 1 - c, y, x, zl)

    def remote(src, dst, ssem, rsem, dev):
        return pltpu.make_async_remote_copy(
            src_ref=src, dst_ref=dst, send_sem=ssem, recv_sem=rsem,
            device_id=dev, device_id_type=MESH,
        )

    def pair_copy(g):
        rows = pl.ds(16 * g, 16)
        return pltpu.make_async_copy(pair_in.at[rows], pair.at[rows], pin.at[g])

    def weight_copy(k):
        src, dst = ((wch, None), (wq_in, wq), (wg_in, wg), (wo_in, wo), (wk_in, wk), (wv_in, wv))[k]
        return pltpu.make_async_copy(src, dst, win.at[k - 1])

    def seq_of(u):
        return 2 * first_chunk(lax.div(u, 2), zh) + lax.rem(u, 2)

    def z_copy(src, dst, ssem, rsem, d, owner):
        return remote(src, dst.at[pl.ds(2 * owner, 2)], ssem.at[d - 1], rsem.at[d - 1], to_z(d))

    dev_swapped = device(y, c, zh, x, zl)
    dev_next, dev_previous = device(y, c, x, zh, zl), device(x, c, zh, y, zl)

    def wide_to(e, d):
        xx, yy = (1 - e) * mod4(x + d) + e * x, e * mod4(y + d) + (1 - e) * y
        return device(zh, c, yy, xx, zl)

    def thin_to(e, k, cross):
        return device(zh, c, (1 - e) * k + e * y, e * k + (1 - e) * x, lax.rem(zl + cross, 2))

    def e_copy(e):
        return remote(
            feat.at[e], ebuf.at[e], vs.at[e], vr.at[e], (dev_swapped, dev_next)[e]
        )

    def y_copy(src, e, d, cross):
        k = thin_at(e)
        here = kv.at[2 * k + e, 2 * wide_at(e) + zl]
        return remote(
            src, here, ys.at[e, d, cross], yr.at[2 * k + e, cross], thin_to(e, mod4(k + d), cross)
        )

    Y_ALL = [(d, cross) for d in (1, 3, 2, 0) for cross in (0, 1) if d or cross]

    def stage_y(src, e):
        for d, cross in Y_ALL:
            y_copy(src, e, d, cross).start()
        kv[2 * thin_at(e) + e, 2 * wide_at(e) + zl] = src[...]

    def y_arrived(u):
        n, e = seq_of(u), lax.rem(u, 2)

        def wait(cross, b):
            here = kv.at[n, b]
            remote(here, here, ys.at[0, 0, cross], yr.at[n, cross], dev_zl).wait_recv()

        pl.when(thin_at(e) != first_chunk(lax.div(u, 2), zh))(
            lambda: wait(0, 2 * wide_at(e) + zl)
        )
        wait(1, 2 * wide_at(e) + 1 - zl)

    def x_copy(u, d, owner):
        here = kv.at[seq_of(u), pl.ds(2 * owner, 2)]
        return remote(here, here, xs.at[u, d - 1], xr.at[u, d - 1], wide_to(lax.rem(u, 2), d))

    def stage_x(u):
        for d in (1, 3, 2):
            x_copy(u, d, wide_at(lax.rem(u, 2))).start()

    def stage_w(u):
        for d in (1, 3, 2):
            x_copy(u, d, mod4(wide_at(lax.rem(u, 2)) - d)).wait_recv()

    barrier = pltpu.get_barrier_semaphore()
    partners = [to_z(d) for d in (1, 2, 3)] + [to_y(d) for d in (1, 2, 3)]
    partners += [device(zh, c, mod4(y + d), x, 1 - zl) for d in (0, 1, 2, 3)]
    partners += [device(zh, c, y, mod4(x + d), 1 - zl) for d in (1, 2, 3)]
    partners += [to_x(d) for d in (1, 2, 3)] + [dev_core]
    for dev in partners:
        pl.semaphore_signal(barrier, inc=1, device_id=dev, device_id_type=MESH)

    @pl.when(off_a != 0)
    def _():
        pl.semaphore_signal(barrier, inc=1, device_id=dev_swapped, device_id_type=MESH)

    @pl.when(off_b != 0)
    def _():
        pl.semaphore_signal(barrier, inc=1, device_id=dev_next, device_id_type=MESH)
        pl.semaphore_signal(barrier, inc=1, device_id=dev_previous, device_id_type=MESH)

    for g in range(4):
        pair_copy(g).start()
    for k in range(1, 6):
        weight_copy(k).start()
    qf[pl.ds(2 * zh, 2)] = feat[...]
    ag[pl.ds(2 * zh, 2)] = adj[...]
    row = lax.broadcasted_iota(jnp.int32, (128, 8), 0)
    col = lax.broadcasted_iota(jnp.int32, (128, 8), 1)
    rep = dot(jnp.where(lax.div(row, 16) == col, 1.0, 0.0).astype(BF16), wch[...])
    spread_map(rep, wexp)
    dbias[...] = jnp.zeros_like(dbias)
    pl.semaphore_wait(barrier, len(partners) + off_a + 2 * off_b)

    @pl.when(off_a == 0)
    def _():
        stage_y(feat.at[0], 0)

    @pl.when(off_a != 0)
    def _():
        e_copy(0).start()

    @pl.when(off_b == 0)
    def _():
        stage_y(feat.at[1], 1)

    @pl.when(off_b != 0)
    def _():
        e_copy(1).start()

    for d in (1, 3, 2):
        z_copy(feat, qf, zs, zr, d, zh).start()

    def bias_group(g):
        pair_copy(g).wait()
        total = jnp.zeros((128, 256), F32)
        for p in range(8):
            i = 16 * g + 2 * p
            both = jnp.concatenate([pair[i], pair[i + 1]], axis=1)
            total += dot(wexp[:, p * 256 : (p + 1) * 256], both, NT)
        for h in range(8):
            bias[c, h * 64 + 16 * g : h * 64 + 16 * g + 16, :] = total[h * 16 : h * 16 + 16]

    bias_group(0)
    bias_group(1)
    bias_group(2)
    y_arrived(0)
    stage_x(0)

    @pl.when(off_b != 0)
    def _():
        e_copy(1).wait_recv()
        stage_y(ebuf.at[1], 1)

    @pl.when(off_a != 0)
    def _():
        e_copy(0).wait_recv()
        stage_y(ebuf.at[0], 0)

    for d in (1, 3, 2):
        z_copy(adj, ag, as_, ar, d, zh).start()
    bias_group(3)
    swap = remote(bias.at[c], bias.at[c], bs, br, dev_core)
    swap.start()
    for k in range(1, 6):
        weight_copy(k).wait()

    lanes = lax.broadcasted_iota(jnp.int32, (64, 256), 1)
    masks = [(lanes >= 32 * h) & (lanes < 32 * h + 32) for h in range(8)]

    def query_side(n):
        rows = qf[n]
        q = (dot(rows, wq[...]) * SCALE).astype(BF16).astype(F32)
        gate = jax.nn.sigmoid(dot(rows, wg[...]) + bg[...])
        dg = dot(ag[n], wo[...], NT)
        da = (dg * gate).astype(BF16).astype(F32)
        fac[n] = dg * gate * (1.0 - gate)
        for h in range(8):
            qbd[n, h * 64 : h * 64 + 64, :] = jnp.where(masks[h], q, 0.0).astype(BF16)
            dabd[n, h * 64 : h * 64 + 64, :] = jnp.where(masks[h], da, 0.0).astype(BF16)
        cw[n, :, 0:512] = dot(qbd[n], wk[...], NT).astype(BF16).T
        cw[n, :, 512:1024] = dot(dabd[n], wv[...], NT).astype(BF16).T

    query_side(seq_of(0))
    query_side(seq_of(1))
    y_arrived(1)
    stage_x(1)
    y_arrived(2)
    stage_x(2)
    y_arrived(3)
    stage_x(3)
    remote(bias.at[1 - c], bias.at[1 - c], bs, br, dev_core).wait_recv()

    lane = lax.broadcasted_iota(jnp.int32, (64, 128), 1)

    def stat_copy(n, d):
        return remote(stout.at[n], stin.at[n, d - 1], ss.at[n, d - 1], sr.at[n, d - 1], to_z(d))

    def first(u):
        n = seq_of(u)
        @pl.when((u >= 2) & (lax.rem(u, 2) == 0))
        def _():
            owner = first_chunk(lax.div(u, 2), zh)
            z_copy(feat, qf, zs, zr, mod4(zh - owner), owner).wait_recv()
            z_copy(adj, ag, as_, ar, mod4(zh - owner), owner).wait_recv()

        @pl.when(u >= 2)
        def _():
            query_side(n)

        stage_w(u)
        rows = kv[n].reshape(512, 256)
        kbuf[n] = dot(rows, wk[...]).astype(BF16)
        vbuf[n] = dot(rows, wv[...]).astype(BF16)
        sbuf[...] = dot(qbd[n], kbuf[n], NT)
        dpbuf[n] = dot(dabd[n], vbuf[n], NT)
        tiles = []
        for h in range(8):
            rows = pl.ds(h * 64, 64)
            s0 = sbuf[rows, 0:256] + bias[0, rows, :]
            s1 = sbuf[rows, 256:512] + bias[1, rows, :]
            top = jnp.max(jnp.maximum(s0, s1), axis=1, keepdims=True)
            p0, p1 = jnp.exp(s0 - top), jnp.exp(s1 - top)
            pbuf[n, rows, 0:256] = p0
            pbuf[n, rows, 256:512] = p1
            total = jnp.sum(p0 + p1, axis=1, keepdims=True)
            mixed = jnp.sum(
                p0 * dpbuf[n, rows, 0:256] + p1 * dpbuf[n, rows, 256:512], axis=1, keepdims=True
            )
            tiles.append(jnp.where(lane == 0, top, jnp.where(lane == 1, total, mixed)))
        stats = jnp.concatenate(tiles, axis=0).T[0:4]
        for k in range(4):
            stout[n, 4 * k : 4 * k + 4, :] = stats[:, 128 * k : 128 * k + 128]
        for d in (1, 3, 2):
            stat_copy(n, d).start()

        @pl.when(u < 4)
        def _():
            y_arrived(u + 4)
            stage_x(u + 4)

    def odd(u):
        return 1 - lax.rem(u, 2)

    def back_seq(u):
        return 2 * second_chunk(lax.div(u, 2), zh) + odd(u)

    def rx_copy(u, d):
        e = odd(u)
        return remote(
            part.at[u, pl.ds(2 * mod4(wide_at(e) + d), 2)], in_x.at[u, d - 1],
            rxs.at[u, d - 1], rxr.at[u, d - 1], wide_to(e, d),
        )

    def ry_copy(u, cross):
        e, k = odd(u), second_chunk(lax.div(u, 2), zh)
        slot = 2 * mod4(thin_at(e) - k) + cross
        return remote(
            hop.at[u, cross], in_y.at[e, slot], rys.at[u, cross], ryr.at[e, slot],
            thin_to(e, k, cross),
        )

    def ry_arrived(e, slot):
        remote(hop.at[0, 0], in_y.at[e, slot], rys.at[0, 0], ryr.at[e, slot], dev_zl).wait_recv()

    def rt_copy(e):
        return remote(
            tout.at[e], tin.at[e], rts.at[e], rtr.at[e], (dev_swapped, dev_previous)[e]
        )

    def rz_copy(u):
        owner = second_chunk(lax.div(u, 2), zh)
        slot = 2 * (mod4(owner - zh) - 1) + odd(u)
        return remote(
            zout.at[u], zin.at[slot], rzs.at[u], rzr.at[slot], device(owner, c, y, x, zl)
        )

    def rz_arrived(slot):
        remote(zout.at[slot], zin.at[slot], rzs.at[slot], rzr.at[slot], to_z(1)).wait_recv()

    def back_x(u):
        for d in (1, 3, 2):
            rx_copy(u, d).start()

    def x_total(u, b):
        mine = part[u, 2 * wide_at(odd(u)) + b]
        return (mine.astype(F32) + in_x[u, 0, b].astype(F32)) + (
            in_x[u, 1, b].astype(F32) + in_x[u, 2, b].astype(F32)
        )

    def back_y(u):
        for d in (1, 3, 2):
            rx_copy(u, d).wait_recv()
        hop[u, 1] = x_total(u, 1 - zl).astype(BF16)
        ry_copy(u, 1).start()
        own = x_total(u, zl)
        away = thin_at(odd(u)) != second_chunk(lax.div(u, 2), zh)

        @pl.when(away)
        def _():
            hop[u, 0] = own.astype(BF16)
            ry_copy(u, 0).start()

        @pl.when(jnp.logical_not(away))
        def _():
            acc[odd(u)] = own

    def back_t(u):
        def finish(e):
            for slot in range(1, 8):
                ry_arrived(e, slot)
            got = [in_y[e, slot].astype(F32) for slot in range(1, 8)]
            total = ((acc[e] + got[0]) + (got[1] + got[2])) + ((got[3] + got[4]) + (got[5] + got[6]))
            acc[e] = total

            @pl.when((off_a, off_b)[e] != 0)
            def _():
                tout[e] = total.astype(BF16)
                rt_copy(e).start()

        k = second_chunk(lax.div(u, 2), zh)
        for e in (0, 1):
            pl.when((odd(u) == e) & (thin_at(e) == k))(lambda: finish(e))

    def second(u):
        n = back_seq(u)
        for d in (1, 3, 2):
            stat_copy(n, d).wait_recv()

        def wide(v):
            return jnp.concatenate([v[4 * k : 4 * k + 4] for k in range(4)], axis=1)

        own_stats = wide(stout[n])
        others = [wide(stin[n, d]) for d in range(3)]
        tops = [own_stats[0:1]] + [o[0:1] for o in others]
        top = jnp.maximum(jnp.maximum(tops[0], tops[1]), jnp.maximum(tops[2], tops[3]))
        own = jnp.exp(tops[0] - top)
        total, mixed = own * own_stats[1:2], own * own_stats[2:3]
        for d in range(3):
            weight = jnp.exp(tops[d + 1] - top)
            total += weight * others[d][1:2]
            mixed += weight * others[d][2:3]
        down = lax.broadcasted_iota(jnp.int32, (128, 512), 0)
        ab = jnp.where(down == 0, own / total, mixed / total).T
        for h in range(8):
            rows = pl.ds(h * 64, 64)
            a = ab[h * 64 : h * 64 + 64, 0:1]
            delta = ab[h * 64 : h * 64 + 64, 1:2]
            for half in (0, 1):
                cols = slice(half * 256, half * 256 + 256)
                probs = pbuf[n, rows, cols] * a
                sp[pl.ds(512 + h * 64, 64), cols] = probs.astype(BF16)
                ds = probs * (dpbuf[n, rows, cols] - delta)
                sp[rows, cols] = ds.astype(BF16)
                dbias[half, rows, :] += ds
        both = dot(cw[n], sp[...]).astype(BF16).T
        part[u] = both.reshape(8, 64, 256)
        back_x(u)
        att_all = dot(sp[512:1024, :], vbuf[n])
        dq_all = dot(sp[0:512, :], kbuf[n])
        att, dq = jnp.zeros((64, 256), F32), jnp.zeros((64, 256), F32)
        for h in range(8):
            att += jnp.where(masks[h], att_all[h * 64 : h * 64 + 64], 0.0)
            dq += jnp.where(masks[h], dq_all[h * 64 : h * 64 + 64], 0.0)
        dq = (dq * SCALE).astype(BF16)
        dgp = (fac[n] * att).astype(BF16)
        ipart[u] = dot(dq, wq[...], NT) + dot(dgp, wg[...], NT)

        @pl.when(u < 6)
        def _():
            zout[u] = ipart[u].astype(BF16)
            rz_copy(u).start()

    LY, LT = LAGS

    def step(t, carry):
        @pl.when(t < 8)
        def _():
            first(t)

        @pl.when(t >= SHIFT)
        def _():
            second(t - SHIFT)

        for lag, stage in ((LY, back_y), (LT, back_t)):
            if lag < 8:
                pl.when(t >= SHIFT + lag)(lambda: stage(t - SHIFT - lag))

        return carry

    lax.fori_loop(0, 8 + SHIFT, step, 0)
    give = remote(dbias.at[1 - c], dbin, es, er, dev_core)
    give.start()
    waits = [(back_y, u, u + LY) for u in range(8)] + [(back_t, u, u + LT) for u in range(8)]
    for fun, u, when in sorted((w for w in waits if w[2] > 7), key=lambda w: w[2]):
        fun(u)
    give.wait_recv()
    dbout[...] = dbias[c] + dbin[...]
    db_copy = pltpu.make_async_copy(dbout, db, pout)
    db_copy.start()
    for u in range(6):
        rz_arrived(u)

    for e in (0, 1):

        @pl.when((off_a, off_b)[e] != 0)
        def _():
            rt_copy(e).wait_recv()
            acc[e] = tin[e].astype(F32)

    for e in (0, 1):
        out[e] = (
            (acc[e] + ipart[7 - e] + zin[e].astype(F32))
            + (zin[2 + e].astype(F32) + zin[4 + e].astype(F32))
        ).astype(BF16)

    for d in (1, 3, 2):
        z_copy(feat, qf, zs, zr, d, zh).wait_send()
        z_copy(adj, ag, as_, ar, d, zh).wait_send()
    swap.wait_send()
    give.wait_send()

    for e in (0, 1):
        for d, cross in Y_ALL:
            y_copy(feat.at[e], e, d, cross).wait_send()

        @pl.when((off_a, off_b)[e] != 0)
        def _():
            e_copy(e).wait_send()
            rt_copy(e).wait_send()

    def drain(u, carry):
        for d in (1, 3, 2):
            x_copy(u, d, wide_at(lax.rem(u, 2))).wait_send()
            stat_copy(u, d).wait_send()
            rx_copy(u, d).wait_send()
        ry_copy(u, 1).wait_send()

        @pl.when(thin_at(odd(u)) != second_chunk(lax.div(u, 2), zh))
        def _():
            ry_copy(u, 0).wait_send()

        @pl.when(u < 6)
        def _():
            rz_copy(u).wait_send()

        return carry

    lax.fori_loop(0, 8, drain, 0)
    db_copy.wait()


def couple_kernel(db, wch, hom, couple, out, wide, store, sems):
    row = lax.broadcasted_iota(jnp.int32, (128, 8), 0)
    col = lax.broadcasted_iota(jnp.int32, (128, 8), 1)
    rep = dot(jnp.where(lax.div(row, 16) == col, 1.0, 0.0).astype(BF16), wch[...])
    spread_map(rep, wide)
    out[...] = hom[...]

    def copy(g):
        rows = pl.ds(8 * g, 8)
        return pltpu.make_async_copy(store.at[rows], couple.at[rows], sems.at[g])

    for g in range(4):
        rows = jnp.concatenate(
            [db[h * 64 + 16 * g : h * 64 + 16 * g + 16, :] for h in range(8)], axis=0
        )
        high = rows.astype(BF16)
        low = (rows - high.astype(F32)).astype(BF16)
        both = jnp.concatenate([high, low], axis=0).T
        for p in range(8):
            w = wide[:, p * 256 : (p + 1) * 256]
            res = dot(both, jnp.concatenate([w, w], axis=0)).astype(BF16)
            store[16 * g + 2 * p] = res[:, 0:128]
            store[16 * g + 2 * p + 1] = res[:, 128:256]
            if p % 4 == 3:
                copy(2 * g + p // 4).start()
    for g in range(8):
        copy(g).wait()


VM = pl.BlockSpec(memory_space=pltpu.VMEM)
HBM = pl.BlockSpec(memory_space=pl.ANY)
DMA = pltpu.SemaphoreType.DMA


def per_device(feat, pair, adj, wq, wk, wv, wg, bg, wch, wo):
    sds, vmem = jax.ShapeDtypeStruct, pltpu.VMEM
    wch = wch.T
    hom, db = pl.pallas_call(
        kernel,
        out_shape=(sds((2, 64, 256), BF16), sds((512, 256), F32)),
        in_specs=[VM, HBM, VM, HBM, HBM, HBM, HBM, VM, VM, HBM],
        out_specs=(VM, HBM),
        scratch_shapes=[vmem((256, 256), BF16)] * 5
        + [
            vmem((64, 256, 128), BF16),
            vmem((8, 64, 256), BF16),
            vmem((8, 64, 256), BF16),
            vmem((8, 8, 64, 256), BF16),
            vmem((2, 512, 256), F32),
            vmem((2, 512, 256), F32),
            vmem((512, 256), F32),
            vmem((8, 512, 512), F32),
            vmem((8, 512, 512), F32),
            vmem((8, 512, 256), BF16),
            vmem((8, 512, 256), BF16),
            vmem((8, 512, 256), BF16),
            vmem((8, 512, 256), BF16),
            vmem((8, 64, 256), F32),
            vmem((512, 512), F32),
            vmem((8, 256, 1024), BF16),
            vmem((1024, 512), BF16),
            vmem((128, 2048), BF16),
            vmem((8, 16, 128), F32),
            vmem((8, 3, 16, 128), F32),
            vmem((512, 256), F32),
            vmem((2, 64, 256), BF16),
            vmem((8, 64, 256), F32),
            vmem((8, 8, 64, 256), BF16),
            vmem((8, 3, 2, 64, 256), BF16),
            vmem((8, 2, 64, 256), BF16),
            vmem((2, 8, 64, 256), BF16),
            vmem((2, 64, 256), F32),
            vmem((2, 64, 256), BF16),
            vmem((2, 64, 256), BF16),
            vmem((6, 64, 256), BF16),
            vmem((6, 64, 256), BF16),
            DMA((5,)), DMA((4,)), DMA,
            DMA((3,)), DMA((3,)), DMA((3,)), DMA((3,)),
            DMA((2,)), DMA((2,)), DMA((2, 4, 2)), DMA((8, 2)), DMA((8, 3)), DMA((8, 3)),
            DMA, DMA, DMA((8, 3)), DMA((8, 3)), DMA, DMA,
            DMA((8, 3)), DMA((8, 3)), DMA((8, 2)), DMA((2, 8)), DMA((2,)), DMA((2,)),
            DMA((6,)), DMA((6,)),
        ],
        compiler_params=pltpu.CompilerParams(
            collective_id=0, has_side_effects=True, vmem_limit_bytes=VMEM_LIMIT
        ),
        name="fused",
    )(feat, pair, adj, wq, wk, wv, wg, bg.reshape(1, 256), wch, wo)
    couple, homolog = pl.pallas_call(
        couple_kernel,
        out_shape=(sds((64, 256, 128), BF16), sds((2, 64, 256), BF16)),
        in_specs=[VM] * 3,
        out_specs=(HBM, VM),
        scratch_shapes=[vmem((128, 2048), BF16), vmem((64, 256, 128), BF16), DMA((8,))],
        compiler_params=pltpu.CompilerParams(vmem_limit_bytes=VMEM_LIMIT),
        name="couple",
    )(db, wch, hom)
    return homolog, couple


def solution(mesh):
    in_specs = (
        P("seq", "res", None), P("res", "seq", None), P("seq", "res", None),
        P(), P(), P(), P(), P(), P(), P(),
    )
    out_specs = (P("seq", "res", None), P("res", "seq", None))
    return jax.shard_map(
        per_device, mesh=mesh, in_specs=in_specs, out_specs=out_specs, check_vma=False
    )
```

```python
import jax
import jax.numpy as jnp
from jax import lax
from jax.experimental import pallas as pl
from jax.experimental.pallas import tpu as pltpu
from jax.sharding import PartitionSpec as P

F32, BF16 = jnp.float32, jnp.bfloat16
MESH = pl.DeviceIdType.MESH
NT = (((1,), (1,)), ((), ()))
TN = (((0,), (0,)), ((), ()))
VMEM_LIMIT = 61 * 1024 * 1024
SCALE = 32**-0.5
LAGS = (3, 5)
SHIFT = 8


def dot(a, b, dims=(((1,), (0,)), ((), ()))):
    return lax.dot_general(a, b, dims, preferred_element_type=F32)


def mod4(v):
    return lax.rem(v + 8, 4)


def first_chunk(p, zh):
    later = lax.div(p + 3, 4)
    return (1 - later) * zh + later * (p - 1 + lax.div(p + 3 - zh, 4))


def second_chunk(p, zh):
    last = lax.div(p, 3)
    return last * zh + (1 - last) * (p + lax.div(p + 4 - zh, 4))


def differ(a, b):
    return lax.div((a - b) * (a - b) + 8, 9)


def spread_map(rep, out):
    row = lax.broadcasted_iota(jnp.int32, (128, 128), 0)
    for i in range(16):
        out[:, i * 128 : (i + 1) * 128] = jnp.where(lax.rem(row, 16) == i, rep, 0.0).astype(BF16)


def kernel(
    feat_in, pair_in, adj_in, wq_in, wk_in, wv_in, wg_in, bg_in, wch_in, wo_in,
    out, db,
    feat, bg, wch, wq, wk, wv, wg, wo, pair, qf, ag, kv, bias, dbias, dbin, pbuf, dpbuf, kbuf, vbuf, qbd, dabd, fac,
    sbuf, cw, sp, wexp, stout, stin, dbout, ebuf, ipart, part, in_x, hop, in_y, acc, tout, tin, zout, zin,
    win, pin, pout, zs, zr, as_, ar, vs, vr, ys, yr, xs, xr, bs, br, ss, sr, es, er,
    rxs, rxr, rys, ryr, rts, rtr, rzs, rzr,
):
    s, r = lax.axis_index("seq"), lax.axis_index("res")
    zh, c = lax.div(s, 2), lax.rem(s, 2)
    y, x, zl = lax.div(r, 8), lax.rem(lax.div(r, 2), 4), lax.rem(r, 2)
    off_a = differ(y, zh)
    off_b = lax.div(differ(x, y) + differ(y, zh) + 1, 2)

    def wide_at(e):
        return (1 - e) * x + e * y

    def thin_at(e):
        return (1 - e) * y + e * x

    def device(zh_, c_, y_, x_, zl_):
        return (zh_ * 2 + c_, y_ * 8 + x_ * 2 + zl_)

    def to_z(d):
        return device(mod4(zh + d), c, y, x, zl)

    def to_y(d):
        return device(zh, c, mod4(y + d), x, zl)

    def to_x(d):
        return device(zh, c, y, mod4(x + d), zl)

    dev_zl = device(zh, c, y, x, 1 - zl)
    dev_core = device(zh, 1 - c, y, x, zl)

    def remote(src, dst, ssem, rsem, dev):
        return pltpu.make_async_remote_copy(
            src_ref=src, dst_ref=dst, send_sem=ssem, recv_sem=rsem,
            device_id=dev, device_id_type=MESH,
        )

    def pair_copy(g):
        rows = pl.ds(16 * g, 16)
        return pltpu.make_async_copy(pair_in.at[rows], pair.at[rows], pin.at[g])

    def weight_copy(k):
        src, dst = (
            (feat_in, feat), (wch_in, wch), (adj_in, ag.at[pl.ds(2 * zh, 2)]), (bg_in, bg),
            (wq_in, wq), (wg_in, wg), (wo_in, wo), (wk_in, wk), (wv_in, wv),
        )[k]
        return pltpu.make_async_copy(src, dst, win.at[k])

    def seq_of(u):
        return 2 * first_chunk(lax.div(u, 2), zh) + lax.rem(u, 2)

    def z_copy(src, dst, ssem, rsem, d, owner):
        return remote(src, dst.at[pl.ds(2 * owner, 2)], ssem.at[d - 1], rsem.at[d - 1], to_z(d))

    dev_swapped = device(y, c, zh, x, zl)
    dev_next, dev_previous = device(y, c, x, zh, zl), device(x, c, zh, y, zl)

    def wide_to(e, d):
        xx, yy = (1 - e) * mod4(x + d) + e * x, e * mod4(y + d) + (1 - e) * y
        return device(zh, c, yy, xx, zl)

    def thin_to(e, k, cross):
        return device(zh, c, (1 - e) * k + e * y, e * k + (1 - e) * x, lax.rem(zl + cross, 2))

    def e_copy(e):
        return remote(
            feat.at[e], ebuf.at[e], vs.at[e], vr.at[e], (dev_swapped, dev_next)[e]
        )

    def y_copy(src, e, d, cross):
        k = thin_at(e)
        here = kv.at[2 * k + e, 2 * wide_at(e) + zl]
        return remote(
            src, here, ys.at[e, d, cross], yr.at[2 * k + e, cross], thin_to(e, mod4(k + d), cross)
        )

    Y_ALL = [(d, cross) for d in (1, 3, 2, 0) for cross in (0, 1) if d or cross]

    def stage_y(src, e):
        for d, cross in Y_ALL:
            y_copy(src, e, d, cross).start()
        kv[2 * thin_at(e) + e, 2 * wide_at(e) + zl] = src[...]

    def y_arrived(u):
        n, e = seq_of(u), lax.rem(u, 2)

        def wait(cross, b):
            here = kv.at[n, b]
            remote(here, here, ys.at[0, 0, cross], yr.at[n, cross], dev_zl).wait_recv()

        pl.when(thin_at(e) != first_chunk(lax.div(u, 2), zh))(
            lambda: wait(0, 2 * wide_at(e) + zl)
        )
        wait(1, 2 * wide_at(e) + 1 - zl)

    def x_copy(u, d, owner):
        here = kv.at[seq_of(u), pl.ds(2 * owner, 2)]
        return remote(here, here, xs.at[u, d - 1], xr.at[u, d - 1], wide_to(lax.rem(u, 2), d))

    def stage_x(u):
        for d in (2, 1, 3):
            x_copy(u, d, wide_at(lax.rem(u, 2))).start()

    def stage_w(u):
        for d in (1, 3, 2):
            x_copy(u, d, mod4(wide_at(lax.rem(u, 2)) - d)).wait_recv()

    barrier = pltpu.get_barrier_semaphore()
    partners = [to_z(d) for d in (1, 2, 3)] + [to_y(d) for d in (1, 2, 3)]
    partners += [device(zh, c, mod4(y + d), x, 1 - zl) for d in (0, 1, 2, 3)]
    partners += [device(zh, c, y, mod4(x + d), 1 - zl) for d in (1, 2, 3)]
    partners += [to_x(d) for d in (1, 2, 3)] + [dev_core]
    for dev in partners:
        pl.semaphore_signal(barrier, inc=1, device_id=dev, device_id_type=MESH)

    @pl.when(off_a != 0)
    def _():
        pl.semaphore_signal(barrier, inc=1, device_id=dev_swapped, device_id_type=MESH)

    @pl.when(off_b != 0)
    def _():
        pl.semaphore_signal(barrier, inc=1, device_id=dev_next, device_id_type=MESH)
        pl.semaphore_signal(barrier, inc=1, device_id=dev_previous, device_id_type=MESH)

    for k in range(4):
        weight_copy(k).start()
    for g in range(4):
        pair_copy(g).start()
    for k in range(4, 9):
        weight_copy(k).start()
    weight_copy(0).wait()
    weight_copy(1).wait()
    qf[pl.ds(2 * zh, 2)] = feat[...]
    row = lax.broadcasted_iota(jnp.int32, (128, 8), 0)
    col = lax.broadcasted_iota(jnp.int32, (128, 8), 1)
    rep = dot(jnp.where(lax.div(row, 16) == col, 1.0, 0.0).astype(BF16), wch[...])
    spread_map(rep, wexp)
    dbias[...] = jnp.zeros_like(dbias)
    pl.semaphore_wait(barrier, len(partners) + off_a + 2 * off_b)

    @pl.when(off_a == 0)
    def _():
        stage_y(feat.at[0], 0)

    @pl.when(off_a != 0)
    def _():
        e_copy(0).start()

    @pl.when(off_b == 0)
    def _():
        stage_y(feat.at[1], 1)

    @pl.when(off_b != 0)
    def _():
        e_copy(1).start()

    for d in (1, 3, 2):
        z_copy(feat, qf, zs, zr, d, zh).start()

    def bias_group(g):
        pair_copy(g).wait()
        total = jnp.zeros((128, 256), F32)
        for p in range(8):
            i = 16 * g + 2 * p
            both = jnp.concatenate([pair[i], pair[i + 1]], axis=1)
            total += dot(wexp[:, p * 256 : (p + 1) * 256], both, NT)
        for h in range(8):
            bias[c, h * 64 + 16 * g : h * 64 + 16 * g + 16, :] = total[h * 16 : h * 16 + 16]

    bias_group(0)
    bias_group(1)
    bias_group(2)
    y_arrived(0)
    stage_x(0)

    @pl.when(off_b != 0)
    def _():
        e_copy(1).wait_recv()
        stage_y(ebuf.at[1], 1)

    @pl.when(off_a != 0)
    def _():
        e_copy(0).wait_recv()
        stage_y(ebuf.at[0], 0)

    weight_copy(2).wait()
    for d in (1, 3, 2):
        z_copy(ag.at[pl.ds(2 * zh, 2)], ag, as_, ar, d, zh).start()
    bias_group(3)
    swap = remote(bias.at[c], bias.at[c], bs, br, dev_core)
    swap.start()
    for k in range(3, 9):
        weight_copy(k).wait()

    lanes = lax.broadcasted_iota(jnp.int32, (64, 256), 1)
    masks = [(lanes >= 32 * h) & (lanes < 32 * h + 32) for h in range(8)]

    def query_side(n):
        rows = qf[n]
        q = (dot(rows, wq[...]) * SCALE).astype(BF16).astype(F32)
        gate = jax.nn.sigmoid(dot(rows, wg[...]) + bg[...])
        dg = dot(ag[n], wo[...], NT)
        da = (dg * gate).astype(BF16).astype(F32)
        fac[n] = dg * gate * (1.0 - gate)
        for h in range(8):
            qbd[n, h * 64 : h * 64 + 64, :] = jnp.where(masks[h], q, 0.0).astype(BF16)
            dabd[n, h * 64 : h * 64 + 64, :] = jnp.where(masks[h], da, 0.0).astype(BF16)
        cw[n, :, 0:512] = dot(qbd[n], wk[...], NT).astype(BF16).T
        cw[n, :, 512:1024] = dot(dabd[n], wv[...], NT).astype(BF16).T

    query_side(seq_of(0))
    query_side(seq_of(1))
    y_arrived(1)
    stage_x(1)
    y_arrived(2)
    stage_x(2)
    y_arrived(3)
    stage_x(3)
    remote(bias.at[1 - c], bias.at[1 - c], bs, br, dev_core).wait_recv()

    lane = lax.broadcasted_iota(jnp.int32, (64, 128), 1)

    def stat_copy(n, d):
        return remote(stout.at[n], stin.at[n, d - 1], ss.at[n, d - 1], sr.at[n, d - 1], to_z(d))

    def first(u):
        n = seq_of(u)
        @pl.when((u >= 2) & (lax.rem(u, 2) == 0))
        def _():
            owner = first_chunk(lax.div(u, 2), zh)
            z_copy(feat, qf, zs, zr, mod4(zh - owner), owner).wait_recv()
            z_copy(ag.at[pl.ds(2 * zh, 2)], ag, as_, ar, mod4(zh - owner), owner).wait_recv()

        @pl.when(u >= 2)
        def _():
            query_side(n)

        stage_w(u)
        rows = kv[n].reshape(512, 256)
        kbuf[n] = dot(rows, wk[...]).astype(BF16)
        vbuf[n] = dot(rows, wv[...]).astype(BF16)
        sbuf[...] = dot(qbd[n], kbuf[n], NT)
        dpbuf[n] = dot(dabd[n], vbuf[n], NT)
        tiles = []
        for h in range(8):
            rows = pl.ds(h * 64, 64)
            s0 = sbuf[rows, 0:256] + bias[0, rows, :]
            s1 = sbuf[rows, 256:512] + bias[1, rows, :]
            top = jnp.max(jnp.maximum(s0, s1), axis=1, keepdims=True)
            p0, p1 = jnp.exp(s0 - top), jnp.exp(s1 - top)
            pbuf[n, rows, 0:256] = p0
            pbuf[n, rows, 256:512] = p1
            total = jnp.sum(p0 + p1, axis=1, keepdims=True)
            mixed = jnp.sum(
                p0 * dpbuf[n, rows, 0:256] + p1 * dpbuf[n, rows, 256:512], axis=1, keepdims=True
            )
            tiles.append(jnp.where(lane == 0, top, jnp.where(lane == 1, total, mixed)))
        stats = jnp.concatenate(tiles, axis=0).T[0:4]
        for k in range(4):
            stout[n, 4 * k : 4 * k + 4, :] = stats[:, 128 * k : 128 * k + 128]
        for d in (1, 3, 2):
            stat_copy(n, d).start()

        @pl.when(u < 4)
        def _():
            y_arrived(u + 4)
            stage_x(u + 4)

    def odd(u):
        return 1 - lax.rem(u, 2)

    def back_seq(u):
        return 2 * second_chunk(lax.div(u, 2), zh) + odd(u)

    def rx_copy(u, d):
        e = odd(u)
        return remote(
            part.at[u, pl.ds(2 * mod4(wide_at(e) + d), 2)], in_x.at[u, d - 1],
            rxs.at[u, d - 1], rxr.at[u, d - 1], wide_to(e, d),
        )

    def ry_copy(u, cross):
        e, k = odd(u), second_chunk(lax.div(u, 2), zh)
        slot = 2 * mod4(thin_at(e) - k) + cross
        return remote(
            hop.at[u, cross], in_y.at[e, slot], rys.at[u, cross], ryr.at[e, slot],
            thin_to(e, k, cross),
        )

    def ry_arrived(e, slot):
        remote(hop.at[0, 0], in_y.at[e, slot], rys.at[0, 0], ryr.at[e, slot], dev_zl).wait_recv()

    def rt_copy(e):
        return remote(
            tout.at[e], tin.at[e], rts.at[e], rtr.at[e], (dev_swapped, dev_previous)[e]
        )

    def rz_copy(u):
        owner = second_chunk(lax.div(u, 2), zh)
        slot = 2 * (mod4(owner - zh) - 1) + odd(u)
        return remote(
            zout.at[u], zin.at[slot], rzs.at[u], rzr.at[slot], device(owner, c, y, x, zl)
        )

    def rz_arrived(slot):
        remote(zout.at[slot], zin.at[slot], rzs.at[slot], rzr.at[slot], to_z(1)).wait_recv()

    def back_x(u):
        for d in (2, 1, 3):
            rx_copy(u, d).start()

    def x_total(u, b):
        mine = part[u, 2 * wide_at(odd(u)) + b]
        return (mine.astype(F32) + in_x[u, 0, b].astype(F32)) + (
            in_x[u, 1, b].astype(F32) + in_x[u, 2, b].astype(F32)
        )

    def back_y(u):
        for d in (1, 3, 2):
            rx_copy(u, d).wait_recv()
        hop[u, 1] = x_total(u, 1 - zl).astype(BF16)
        ry_copy(u, 1).start()
        own = x_total(u, zl)
        away = thin_at(odd(u)) != second_chunk(lax.div(u, 2), zh)

        @pl.when(away)
        def _():
            hop[u, 0] = own.astype(BF16)
            ry_copy(u, 0).start()

        @pl.when(jnp.logical_not(away))
        def _():
            acc[odd(u)] = own

    def back_t(u):
        def finish(e):
            for slot in range(1, 8):
                ry_arrived(e, slot)
            got = [in_y[e, slot].astype(F32) for slot in range(1, 8)]
            total = ((acc[e] + got[0]) + (got[1] + got[2])) + ((got[3] + got[4]) + (got[5] + got[6]))
            acc[e] = total

            @pl.when((off_a, off_b)[e] != 0)
            def _():
                tout[e] = total.astype(BF16)
                rt_copy(e).start()

        k = second_chunk(lax.div(u, 2), zh)
        for e in (0, 1):
            pl.when((odd(u) == e) & (thin_at(e) == k))(lambda: finish(e))

    def second(u):
        n = back_seq(u)
        for d in (1, 3, 2):
            stat_copy(n, d).wait_recv()

        def wide(v):
            return jnp.concatenate([v[4 * k : 4 * k + 4] for k in range(4)], axis=1)

        own_stats = wide(stout[n])
        others = [wide(stin[n, d]) for d in range(3)]
        tops = [own_stats[0:1]] + [o[0:1] for o in others]
        top = jnp.maximum(jnp.maximum(tops[0], tops[1]), jnp.maximum(tops[2], tops[3]))
        own = jnp.exp(tops[0] - top)
        total, mixed = own * own_stats[1:2], own * own_stats[2:3]
        for d in range(3):
            weight = jnp.exp(tops[d + 1] - top)
            total += weight * others[d][1:2]
            mixed += weight * others[d][2:3]
        down = lax.broadcasted_iota(jnp.int32, (128, 512), 0)
        ab = jnp.where(down == 0, own / total, mixed / total).T
        for h in range(8):
            rows = pl.ds(h * 64, 64)
            a = ab[h * 64 : h * 64 + 64, 0:1]
            delta = ab[h * 64 : h * 64 + 64, 1:2]
            for half in (0, 1):
                cols = slice(half * 256, half * 256 + 256)
                probs = pbuf[n, rows, cols] * a
                sp[pl.ds(512 + h * 64, 64), cols] = probs.astype(BF16)
                ds = probs * (dpbuf[n, rows, cols] - delta)
                sp[rows, cols] = ds.astype(BF16)
                dbias[half, rows, :] += ds
        both = dot(cw[n], sp[...]).astype(BF16).T
        part[u] = both.reshape(8, 64, 256)
        back_x(u)
        att_all = dot(sp[512:1024, :], vbuf[n])
        dq_all = dot(sp[0:512, :], kbuf[n])
        att, dq = jnp.zeros((64, 256), F32), jnp.zeros((64, 256), F32)
        for h in range(8):
            att += jnp.where(masks[h], att_all[h * 64 : h * 64 + 64], 0.0)
            dq += jnp.where(masks[h], dq_all[h * 64 : h * 64 + 64], 0.0)
        dq = (dq * SCALE).astype(BF16)
        dgp = (fac[n] * att).astype(BF16)
        ipart[u] = dot(dq, wq[...], NT) + dot(dgp, wg[...], NT)

        @pl.when(u < 6)
        def _():
            zout[u] = ipart[u].astype(BF16)
            rz_copy(u).start()

    LY, LT = LAGS

    def step(t, carry):
        @pl.when(t < 8)
        def _():
            first(t)

        @pl.when(t >= SHIFT)
        def _():
            second(t - SHIFT)

        for lag, stage in ((LY, back_y), (LT, back_t)):
            if lag < 8:
                pl.when(t >= SHIFT + lag)(lambda: stage(t - SHIFT - lag))

        return carry

    lax.fori_loop(0, 8 + SHIFT, step, 0)
    give = remote(dbias.at[1 - c], dbin, es, er, dev_core)
    give.start()
    waits = [(back_y, u, u + LY) for u in range(8)] + [(back_t, u, u + LT) for u in range(8)]
    for fun, u, when in sorted((w for w in waits if w[2] > 7), key=lambda w: w[2]):
        fun(u)
    give.wait_recv()
    dbout[...] = dbias[c] + dbin[...]
    db_copy = pltpu.make_async_copy(dbout, db, pout)
    db_copy.start()
    for u in range(6):
        rz_arrived(u)

    for e in (0, 1):

        @pl.when((off_a, off_b)[e] != 0)
        def _():
            rt_copy(e).wait_recv()
            acc[e] = tin[e].astype(F32)

    for e in (0, 1):
        out[e] = (
            (acc[e] + ipart[7 - e] + zin[e].astype(F32))
            + (zin[2 + e].astype(F32) + zin[4 + e].astype(F32))
        ).astype(BF16)

    for d in (1, 3, 2):
        z_copy(feat, qf, zs, zr, d, zh).wait_send()
        z_copy(ag.at[pl.ds(2 * zh, 2)], ag, as_, ar, d, zh).wait_send()
    swap.wait_send()
    give.wait_send()

    for e in (0, 1):
        for d, cross in Y_ALL:
            y_copy(feat.at[e], e, d, cross).wait_send()

        @pl.when((off_a, off_b)[e] != 0)
        def _():
            e_copy(e).wait_send()
            rt_copy(e).wait_send()

    def drain(u, carry):
        for d in (1, 3, 2):
            x_copy(u, d, wide_at(lax.rem(u, 2))).wait_send()
            stat_copy(u, d).wait_send()
            rx_copy(u, d).wait_send()
        ry_copy(u, 1).wait_send()

        @pl.when(thin_at(odd(u)) != second_chunk(lax.div(u, 2), zh))
        def _():
            ry_copy(u, 0).wait_send()

        @pl.when(u < 6)
        def _():
            rz_copy(u).wait_send()

        return carry

    lax.fori_loop(0, 8, drain, 0)
    db_copy.wait()


def couple_kernel(db, wch, hom, couple, out, wide, store, sems):
    row = lax.broadcasted_iota(jnp.int32, (128, 8), 0)
    col = lax.broadcasted_iota(jnp.int32, (128, 8), 1)
    rep = dot(jnp.where(lax.div(row, 16) == col, 1.0, 0.0).astype(BF16), wch[...])
    spread_map(rep, wide)
    out[...] = hom[...]

    def copy(g):
        rows = pl.ds(8 * g, 8)
        return pltpu.make_async_copy(store.at[rows], couple.at[rows], sems.at[g])

    for g in range(4):
        rows = jnp.concatenate(
            [db[h * 64 + 16 * g : h * 64 + 16 * g + 16, :] for h in range(8)], axis=0
        )
        high = rows.astype(BF16)
        low = (rows - high.astype(F32)).astype(BF16)
        both = jnp.concatenate([high, low], axis=0).T
        for p in range(8):
            w = wide[:, p * 256 : (p + 1) * 256]
            res = dot(both, jnp.concatenate([w, w], axis=0)).astype(BF16)
            store[16 * g + 2 * p] = res[:, 0:128]
            store[16 * g + 2 * p + 1] = res[:, 128:256]
            if p % 4 == 3:
                copy(2 * g + p // 4).start()
    for g in range(8):
        copy(g).wait()


VM = pl.BlockSpec(memory_space=pltpu.VMEM)
HBM = pl.BlockSpec(memory_space=pl.ANY)
DMA = pltpu.SemaphoreType.DMA


def per_device(feat, pair, adj, wq, wk, wv, wg, bg, wch, wo):
    sds, vmem = jax.ShapeDtypeStruct, pltpu.VMEM
    wch = wch.T
    hom, db = pl.pallas_call(
        kernel,
        out_shape=(sds((2, 64, 256), BF16), sds((512, 256), F32)),
        in_specs=[HBM] * 10,
        out_specs=(VM, HBM),
        scratch_shapes=[vmem((2, 64, 256), BF16), vmem((1, 256), F32), vmem((8, 128), BF16)]
        + [vmem((256, 256), BF16)] * 5
        + [
            vmem((64, 256, 128), BF16),
            vmem((8, 64, 256), BF16),
            vmem((8, 64, 256), BF16),
            vmem((8, 8, 64, 256), BF16),
            vmem((2, 512, 256), F32),
            vmem((2, 512, 256), F32),
            vmem((512, 256), F32),
            vmem((8, 512, 512), F32),
            vmem((8, 512, 512), F32),
            vmem((8, 512, 256), BF16),
            vmem((8, 512, 256), BF16),
            vmem((8, 512, 256), BF16),
            vmem((8, 512, 256), BF16),
            vmem((8, 64, 256), F32),
            vmem((512, 512), F32),
            vmem((8, 256, 1024), BF16),
            vmem((1024, 512), BF16),
            vmem((128, 2048), BF16),
            vmem((8, 16, 128), F32),
            vmem((8, 3, 16, 128), F32),
            vmem((512, 256), F32),
            vmem((2, 64, 256), BF16),
            vmem((8, 64, 256), F32),
            vmem((8, 8, 64, 256), BF16),
            vmem((8, 3, 2, 64, 256), BF16),
            vmem((8, 2, 64, 256), BF16),
            vmem((2, 8, 64, 256), BF16),
            vmem((2, 64, 256), F32),
            vmem((2, 64, 256), BF16),
            vmem((2, 64, 256), BF16),
            vmem((6, 64, 256), BF16),
            vmem((6, 64, 256), BF16),
            DMA((9,)), DMA((4,)), DMA,
            DMA((3,)), DMA((3,)), DMA((3,)), DMA((3,)),
            DMA((2,)), DMA((2,)), DMA((2, 4, 2)), DMA((8, 2)), DMA((8, 3)), DMA((8, 3)),
            DMA, DMA, DMA((8, 3)), DMA((8, 3)), DMA, DMA,
            DMA((8, 3)), DMA((8, 3)), DMA((8, 2)), DMA((2, 8)), DMA((2,)), DMA((2,)),
            DMA((6,)), DMA((6,)),
        ],
        compiler_params=pltpu.CompilerParams(
            collective_id=0, has_side_effects=True, vmem_limit_bytes=VMEM_LIMIT
        ),
        name="fused",
    )(feat, pair, adj, wq, wk, wv, wg, bg.reshape(1, 256), wch, wo)
    couple, homolog = pl.pallas_call(
        couple_kernel,
        out_shape=(sds((64, 256, 128), BF16), sds((2, 64, 256), BF16)),
        in_specs=[VM] * 3,
        out_specs=(HBM, VM),
        scratch_shapes=[vmem((128, 2048), BF16), vmem((64, 256, 128), BF16), DMA((8,))],
        compiler_params=pltpu.CompilerParams(vmem_limit_bytes=VMEM_LIMIT),
        name="couple",
    )(db, wch, hom)
    return homolog, couple


def solution(mesh):
    in_specs = (
        P("seq", "res", None), P("res", "seq", None), P("seq", "res", None),
        P(), P(), P(), P(), P(), P(), P(),
    )
    out_specs = (P("seq", "res", None), P("res", "seq", None))
    return jax.shard_map(
        per_device, mesh=mesh, in_specs=in_specs, out_specs=out_specs, check_vma=False
    )
```
